1024 devices in a mesh: shot: 16 (over y_lo, x), dom: 64 (over z, y_hi, core).
Axes of the slice: x: 8, y: 8 (y_hi: 4, y_lo: 2; y = y_hi * 2 + y_lo), z: 8, core: 2. Of those that a mesh axis runs over, the one named last changes fastest.
Arguments:
- stiffness: float32 [512, 64, 128], P('dom'), may hold values from 0.04 to 0.16
- buoyancy: float32 [512, 64, 128], P('dom'), may hold values from 0.6 to 1.2
- forward_now: float32 [16, 512, 64, 128], P('shot', 'dom'), may hold values from -3 to 3
- forward_prior: float32 [16, 512, 64, 128], P('shot', 'dom'), may hold values from -3 to 3
- adjoint_now: float32 [16, 512, 64, 128], P('shot', 'dom'), may hold values from -3 to 3
- adjoint_after: float32 [16, 512, 64, 128], P('shot', 'dom'), may hold values from -3 to 3
- source_cells: int32 [16], P('shot'), may hold values from 0 to 4194303
- wavelet: float32 [16, 1], P('shot'), may hold values from -500 to 500
- receiver_cells: int32 [16, 256], P('shot'), may hold values from 0 to 4194303
- residuals: float32 [16, 2, 256], P('shot'), may hold values from -60 to 60
Outputs:
- gradient: float32 [512, 64, 128], P('dom')
The draws below stay inside these ranges and needn't reach their ends.
Inputs may be any that keep to these rules, and one draw needn't show every extreme that they name: `source_cells`: a flat cell index of the grid. `receiver_cells`: flat cell indices of the grid; a cell may repeat.
All inputs are finite; a program needn't handle non-finite values.
Results may differ from the reference program's by a relative error of at most 0.0003.
Values sent between devices are 32-bit elements; how exact they have to be, the bound alone decides.
A program may use at most 64 MiB of HBM per device.

```python
import jax
import jax.numpy as jnp
from jax import lax

NX = 64
NY = 128
STEPS = 2
RECV = 256
SHOTS = 16
NZ = 512


def with_ends(drawn, key, low, largest):
    place = [jax.random.randint(jax.random.fold_in(key, axis), (), 0, length) for axis, length in enumerate(drawn.shape)]
    widest = drawn.shape.index(max(drawn.shape))
    next_to = place[:widest] + [(place[widest] + 1) % drawn.shape[widest]] + place[widest + 1:]
    return drawn.at[tuple(place)].set(low).at[tuple(next_to)].set(largest)


def block_scale(stream_key, shape, pieces, low, high):
    gain, own = 1.0, jax.random.fold_in(stream_key, 6)
    for axis_at, parts in pieces:
        steps = jnp.exp(jax.random.uniform(jax.random.fold_in(own, axis_at), (parts,), jnp.float32, low / len(pieces), high / len(pieces)))
        gain = gain * jnp.repeat(steps, shape[axis_at] // parts).reshape([-1 if axis == axis_at else 1 for axis in range(len(shape))])
    return gain


def centred(rng, shape, scale, limit, shards=(), kind=jnp.bfloat16):
    array = jax.random.normal(rng, shape, jnp.float32) * scale
    if len(shards) > 0:
        array = block_scale(rng, shape, shards, -0.22, 0.18) * array
    return jnp.clip(array, min=-limit, max=limit).astype(kind)


def setup_inputs(seed: int = 0) -> dict:
    key_list = jax.random.split(jax.random.key(seed), 11)
    return {
        "stiffness": jnp.clip(0.04 + 0.12 * jax.random.uniform(key_list[0], (NZ, NX, NY), jnp.float32) ** block_scale(key_list[0], (NZ, NX, NY), ((0, 64),), -0.2, 0.2), 0.04, 0.16),
        "buoyancy": jnp.clip(0.6 + 0.6 * jax.random.uniform(key_list[1], (NZ, NX, NY), jnp.float32) ** block_scale(key_list[1], (NZ, NX, NY), ((0, 64),), -0.2, 0.2), 0.6, 1.2),
        "forward_now": centred(key_list[2], (SHOTS, NZ, NX, NY), 0.5, 3.0, ((0, 16), (1, 64)), jnp.float32),
        "forward_prior": centred(key_list[3], (SHOTS, NZ, NX, NY), 0.5, 3.0, ((0, 16), (1, 64)), jnp.float32),
        "adjoint_now": centred(key_list[4], (SHOTS, NZ, NX, NY), 0.5, 3.0, ((0, 16), (1, 64)), jnp.float32),
        "adjoint_after": centred(key_list[5], (SHOTS, NZ, NX, NY), 0.5, 3.0, ((0, 16), (1, 64)), jnp.float32),
        "source_cells": with_ends(jax.random.randint(key_list[6], (SHOTS,), 0, NX * NY * NZ), jax.random.fold_in(key_list[6], 1), 0, (NX * NY * NZ) - 1).astype(jnp.int32),
        "wavelet": centred(key_list[7], (SHOTS, STEPS - 1), 150.0, 500.0, ((0, 16),), jnp.float32),
        "receiver_cells": with_ends(jax.random.randint(key_list[8], (SHOTS, RECV), 0, NX * NY * NZ), jax.random.fold_in(key_list[8], 1), 0, (NX * NY * NZ) - 1).astype(jnp.int32),
        "residuals": centred(key_list[9], (SHOTS, STEPS, RECV), 15.0, 60.0, ((0, 16),), jnp.float32),
    }


C_SECOND = (-205.0 / 72.0, 8.0 / 5.0, -1.0 / 5.0, 8.0 / 315.0, -1.0 / 560.0)
C_FIRST = (4.0 / 5.0, -1.0 / 5.0, 4.0 / 105.0, -1.0 / 280.0)


def window(padded, dimension, shift):
    depth = padded.shape[0] - 8
    width_x = padded.shape[1] - 8
    width_y = padded.shape[2] - 8
    starts = [4, 4, 4]
    starts[dimension] = starts[dimension] + shift
    return padded[starts[0]:starts[0] + depth, starts[1]:starts[1] + width_x, starts[2]:starts[2] + width_y]


def operate(field, buoy_pad):
    field_pad = jnp.pad(field, ((0, 0), (4, 4), (4, 4)))
    curvature = 3.0 * C_SECOND[0] * window(field_pad, 0, 0)
    products = jnp.zeros_like(curvature)
    for dimension in range(3):
        slope_field = jnp.zeros_like(curvature)
        slope_buoy = jnp.zeros_like(curvature)
        for offset in range(1, 5):
            curvature = curvature + C_SECOND[offset] * (window(field_pad, dimension, offset) + window(field_pad, dimension, -offset))
            slope_field = slope_field + C_FIRST[offset - 1] * (window(field_pad, dimension, offset) - window(field_pad, dimension, -offset))
            slope_buoy = slope_buoy + C_FIRST[offset - 1] * (window(buoy_pad, dimension, offset) - window(buoy_pad, dimension, -offset))
        products = products + slope_field * slope_buoy
    return window(buoy_pad, 0, 0) * curvature + products


def inject(field, first_plane, cells, amounts):
    depth = field.shape[0]
    plane_size = field.shape[1] * field.shape[2]
    local_cells = cells - first_plane * plane_size
    inside = (local_cells >= 0) & (local_cells < depth * plane_size)
    local_cells = jnp.where(inside, local_cells, depth * plane_size).astype(jnp.int32)
    flat = field.reshape(-1).at[local_cells].add(amounts, mode="drop")
    return flat.reshape(field.shape)


def reference(stiffness, buoyancy, forward_now, forward_prior, adjoint_now, adjoint_after, source_cells, wavelet, receiver_cells, residuals):
    buoy_ext = jnp.pad(buoyancy, ((4, 4), (4, 4), (4, 4)), mode="edge")

    def zero_pad(field):
        return jnp.pad(field, ((4, 4), (0, 0), (0, 0)))

    def one_shot(items):
        field, earlier, adjoint, after, source, amplitudes, receivers, traces = items
        source = source.reshape(1)
        images = []
        for step in range(STEPS):
            image = operate(zero_pad(field), buoy_ext)
            images.append(image)
            if step + 1 < STEPS:
                advanced = 2.0 * field - earlier + stiffness * image
                advanced = inject(advanced, 0, source, amplitudes[step:step + 1])
                earlier, field = field, advanced
        gradient = jnp.zeros_like(stiffness)
        for step in range(STEPS):
            retreated = 2.0 * adjoint - after + operate(zero_pad(stiffness * adjoint), buoy_ext)
            retreated = inject(retreated, 0, receivers, traces[step])
            after, adjoint = adjoint, retreated
            gradient = gradient + adjoint * images[STEPS - 1 - step]
        return gradient

    per_shot = lax.map(one_shot, (forward_now, forward_prior, adjoint_now, adjoint_after, source_cells, wavelet, receiver_cells, residuals))
    return jnp.sum(per_shot, axis=0)
```

```python
import jax
import jax.numpy as jnp
from jax import lax
from jax.experimental import pallas as pl
from jax.experimental.pallas import tpu as pltpu
from jax.sharding import PartitionSpec as P

C_SECOND = (-205.0 / 72.0, 8.0 / 5.0, -1.0 / 5.0, 8.0 / 315.0, -1.0 / 560.0)
C_FIRST = (4.0 / 5.0, -1.0 / 5.0, 4.0 / 105.0, -1.0 / 280.0)
MESH = pl.DeviceIdType.MESH
WIDTH = 4
PAD = 8
P_NOW, SQ_NOW, P_NEXT, SQ_NEXT = range(4)


def make_kernel(shots, doms, depth, rows, lanes, receivers):
    plane = rows * lanes
    half = depth // 2
    chunk = half * rows // shots
    per_plane = rows // chunk
    inside = pl.ds(PAD, rows)

    def kernel(
        stiff_hbm,
        buoy_hbm,
        now_hbm,
        prior_hbm,
        adj_hbm,
        after_hbm,
        source_ref,
        wavelet_ref,
        cells_ref,
        traces_ref,
        out_ref,
        buoy,
        fields,
        stiff,
        prior,
        adj,
        after,
        far_halo,
        near_halo,
        slopes,
        base,
        slope_z,
        image,
        adj_next,
        injected,
        grad,
        parts,
        sums,
        load_sem,
        halo_send,
        halo_recv,
        part_send,
        part_recv,
        sum_send,
        sum_recv,
    ):
        shot = lax.axis_index("shot")
        dom = lax.axis_index("dom")
        core = lax.rem(dom, 2)
        near = dom + 1 - 2 * core
        far = dom - 1 + 2 * core
        has_far = (far >= 0) & (far < doms)
        far_count = jnp.where(has_far, 1, 0)
        outer = core * half
        inner = half - outer
        side = (2 * core - 1).astype(jnp.float32)

        barrier = pltpu.get_barrier_semaphore()
        peers = sorted(range(1, shots), key=lambda i: -min(i % 8, 8 - i % 8))

        @pl.when(has_far)
        def _():
            pl.semaphore_signal(barrier, 1, device_id={"dom": far}, device_id_type=MESH)

        pl.semaphore_signal(barrier, 1, device_id={"dom": near}, device_id_type=MESH)
        for i in peers:
            pl.semaphore_signal(
                barrier, 1, device_id={"shot": lax.rem(shot + i, shots)}, device_id_type=MESH
            )

        loads = [
            pltpu.make_async_copy(src, dst, load_sem.at[i])
            for i, (src, dst) in enumerate(
                (
                    (buoy_hbm, buoy.at[pl.ds(WIDTH, depth), inside]),
                    (now_hbm.at[0], fields.at[P_NOW, pl.ds(WIDTH, depth), inside]),
                    (stiff_hbm, stiff),
                    (adj_hbm.at[0], adj),
                    (prior_hbm.at[0], prior),
                    (after_hbm.at[0], after),
                )
            )
        ]
        for load in loads:
            load.start()

        margin = jnp.zeros((PAD, lanes), jnp.float32)
        blank = jnp.zeros((rows, lanes), jnp.float32)

        def clear(f, carry):
            for z in range(WIDTH):
                fields[f, z, inside] = blank
                fields[f, WIDTH + depth + z, inside] = blank
            for z in range(depth):
                fields[f, WIDTH + z, 0:PAD] = margin
                fields[f, WIDTH + z, PAD + rows : 2 * PAD + rows] = margin
            return carry

        lax.fori_loop(0, 4, clear, 0)

        loads[2].wait()
        loads[3].wait()

        def scale(z, carry):
            fields[SQ_NOW, WIDTH + z, inside] = stiff[z] * adj[z]
            return carry

        lax.fori_loop(0, depth, scale, 0)
        loads[0].wait()
        loads[1].wait()

        def far_copy(f):
            if f == 4:
                src = buoy.at[pl.ds(WIDTH + outer, half), inside]
                dst = buoy.at[pl.ds((1 - core) * (WIDTH + depth), half), inside]
            else:
                src = fields.at[f, pl.ds(WIDTH + outer, half), inside]
                dst = far_halo.at[f]
            return pltpu.make_async_remote_copy(
                src, dst, halo_send.at[0, f], halo_recv.at[0, f], device_id={"dom": far}, device_id_type=MESH
            )

        def far_arrival(f):
            if f == 4:
                dst = buoy.at[pl.ds(core * (WIDTH + depth), half), inside]
            else:
                dst = far_halo.at[f]
            return pltpu.make_async_remote_copy(
                dst, dst, halo_send.at[0, f], halo_recv.at[0, f], device_id={"dom": far}, device_id_type=MESH
            )

        def near_copy(f):
            if f == 4:
                src = buoy.at[pl.ds(WIDTH + inner, half), inside]
                dst = buoy.at[pl.ds(core * (WIDTH + depth), half), inside]
            else:
                src = fields.at[f, pl.ds(WIDTH + inner, half), inside]
                dst = near_halo.at[f]
            return pltpu.make_async_remote_copy(
                src, dst, halo_send.at[1, f], halo_recv.at[1, f], device_id={"dom": near}, device_id_type=MESH
            )

        def near_arrival(f):
            if f == 4:
                dst = buoy.at[pl.ds((1 - core) * (WIDTH + depth), half), inside]
            else:
                dst = near_halo.at[f]
            return pltpu.make_async_remote_copy(
                dst, dst, halo_send.at[1, f], halo_recv.at[1, f], device_id={"dom": near}, device_id_type=MESH
            )

        def when_far(act):
            pl.when(has_far)(act)

        pl.semaphore_wait(barrier, shots + far_count)

        for f in (4, P_NOW, SQ_NOW):
            when_far(far_copy(f).start)
        for f in (4, P_NOW, SQ_NOW):
            near_copy(f).start()

        @pl.when(jnp.logical_not(has_far))
        def _():
            edge = buoy[WIDTH + core * (depth - 1), inside]
            for z in range(half):
                buoy[core * (WIDTH + depth) + z, inside] = edge
                for f in range(4):
                    far_halo[f, z] = blank

        lane = lax.broadcasted_iota(jnp.int32, (rows, lanes), 1)

        def buoy_slopes(z, carry):
            here = buoy[WIDTH + z, inside]
            buoy[WIDTH + z, 0:PAD] = jnp.broadcast_to(here[0:1], (PAD, lanes))
            buoy[WIDTH + z, PAD + rows : 2 * PAD + rows] = jnp.broadcast_to(
                here[rows - 1 : rows], (PAD, lanes)
            )
            low = jnp.broadcast_to(here[:, 0:1], (rows, lanes))
            high = jnp.broadcast_to(here[:, lanes - 1 : lanes], (rows, lanes))
            along_x = jnp.zeros_like(here)
            along_y = jnp.zeros_like(here)
            for k in range(1, 5):
                up = buoy[WIDTH + z, PAD + k : PAD + k + rows]
                down = buoy[WIDTH + z, PAD - k : PAD - k + rows]
                along_x = along_x + C_FIRST[k - 1] * (up - down)
                up = jnp.where(lane < lanes - k, pltpu.roll(here, lanes - k, 1), high)
                down = jnp.where(lane >= k, pltpu.roll(here, k, 1), low)
                along_y = along_y + C_FIRST[k - 1] * (up - down)
            slopes[0, z] = along_x
            slopes[1, z] = along_y
            return carry

        lax.fori_loop(0, depth, buoy_slopes, 0)

        def buoy_slope_z(start):
            def body(j, carry):
                z = start + j
                along_z = jnp.zeros((rows, lanes), jnp.float32)
                for k in range(1, 5):
                    up = buoy[WIDTH + z + k, inside]
                    down = buoy[WIDTH + z - k, inside]
                    along_z = along_z + C_FIRST[k - 1] * (up - down)
                slopes[2, z] = along_z
                return carry

            lax.fori_loop(0, half, body, 0)

        def local(f):
            def body(z, carry):
                here = fields[f, WIDTH + z, inside]
                curve = 3.0 * C_SECOND[0] * here
                along = jnp.zeros_like(here)
                for k in range(1, 5):
                    up = fields[f, WIDTH + z + k, inside]
                    down = fields[f, WIDTH + z - k, inside]
                    curve = curve + C_SECOND[k] * (up + down)
                    along = along + C_FIRST[k - 1] * (up - down)
                slope_z[f, z] = along
                along = jnp.zeros_like(here)
                for k in range(1, 5):
                    up = fields[f, WIDTH + z, PAD + k : PAD + k + rows]
                    down = fields[f, WIDTH + z, PAD - k : PAD - k + rows]
                    curve = curve + C_SECOND[k] * (up + down)
                    along = along + C_FIRST[k - 1] * (up - down)
                products = along * slopes[0, z]
                along = jnp.zeros_like(here)
                for k in range(1, 5):
                    up = jnp.where(lane < lanes - k, pltpu.roll(here, lanes - k, 1), 0.0)
                    down = jnp.where(lane >= k, pltpu.roll(here, k, 1), 0.0)
                    curve = curve + C_SECOND[k] * (up + down)
                    along = along + C_FIRST[k - 1] * (up - down)
                products = products + along * slopes[1, z]
                base[f, z] = buoy[WIDTH + z, inside] * curve + products
                return carry

            lax.fori_loop(0, depth, body, 0)

        def whole(f, j, is_far):
            halo = far_halo if is_far else near_halo
            up = core if is_far else 1 - core
            z = up * (depth - 1 - j) + (1 - up) * j
            curve = jnp.zeros((rows, lanes), jnp.float32)
            along = jnp.zeros((rows, lanes), jnp.float32)
            for k in range(j + 1, 5):
                m = k - j
                plane_at = up * (m - 1) + (1 - up) * (half - m)
                value = halo[f, plane_at]
                curve = curve + C_SECOND[k] * value
                along = along + C_FIRST[k - 1] * value
            sign = side if is_far else -side
            along = slope_z[f, z] + sign * along
            return z, base[f, z] + buoy[WIDTH + z, inside] * curve + along * slopes[2, z]

        local_source = source_ref[0] - dom * (depth * plane)
        amplitude = wavelet_ref[0, 0]
        cell = lax.broadcasted_iota(jnp.int32, (rows, lanes), 0) * lanes + lane

        def forward(is_far):
            for j in range(half):
                z, value = whole(P_NOW, j, is_far)
                image[z] = value
                shown = jnp.where(cell + z * plane == local_source, amplitude, 0.0)
                fields[P_NEXT, WIDTH + z, inside] = (
                    2.0 * fields[P_NOW, WIDTH + z, inside] - prior[z] + stiff[z] * value + shown
                )

        def backward(is_far):
            for j in range(half):
                z, value = whole(SQ_NOW, j, is_far)
                value = 2.0 * adj[z] - after[z] + value + injected[z, :, 0:lanes]
                adj_next[z] = value
                fields[SQ_NEXT, WIDTH + z, inside] = stiff[z] * value

        def finish(is_far):
            for j in range(half):
                z, last_image = whole(P_NEXT, j, is_far)
                _, value = whole(SQ_NEXT, j, is_far)
                newer = adj_next[z]
                value = 2.0 * newer - adj[z] + value + injected[z, :, lanes : 2 * lanes]
                grad[z] = newer * last_image + value * image[z]

        local_cells = cells_ref[...] - dom * (depth * plane)
        cell_rows = jnp.right_shift(local_cells, 7)
        cell_lanes = jnp.bitwise_and(local_cells, lanes - 1)
        lane_hot = lax.broadcasted_iota(jnp.int32, (lanes, receivers), 0) == cell_lanes
        amounts = jnp.concatenate(
            [jnp.where(lane_hot, traces_ref[0, k : k + 1, :], 0.0) for k in range(2)], axis=0
        )
        high = amounts.astype(jnp.bfloat16)
        rest = amounts - high.astype(jnp.float32)
        middle = rest.astype(jnp.bfloat16)
        low = (rest - middle.astype(jnp.float32)).astype(jnp.bfloat16)

        def inject(z, carry):
            row = lax.broadcasted_iota(jnp.int32, (rows, receivers), 0) + z * rows
            row_hot = jnp.where(row == cell_rows, 1.0, 0.0).astype(jnp.bfloat16)
            total = jnp.zeros((rows, 2 * lanes), jnp.float32)
            for part in (low, middle, high):
                total = total + lax.dot_general(
                    row_hot, part, (((1,), (1,)), ((), ())), preferred_element_type=jnp.float32
                )
            injected[z] = total
            return carry

        def reduce_start(h, start):
            for i in peers:
                peer = lax.rem(shot + i, shots)
                src = grad.at[start + peer // per_plane, pl.ds(lax.rem(peer, per_plane) * chunk, chunk)]
                pltpu.make_async_remote_copy(
                    src, parts.at[h, shot], part_send.at[h, i], part_recv.at[h, i],
                    device_id={"shot": peer}, device_id_type=MESH,
                ).start()

        def reduce_finish(h, start):
            total = grad[start + shot // per_plane, pl.ds(lax.rem(shot, per_plane) * chunk, chunk)]
            for i in peers:
                peer = lax.rem(shot + shots - i, shots)
                pltpu.make_async_remote_copy(
                    parts.at[h, peer], parts.at[h, peer], part_send.at[h, i], part_recv.at[h, i],
                    device_id={"shot": peer}, device_id_type=MESH,
                ).wait_recv()
                total = total + parts[h, peer]
            sums[h] = total
            dst = out_ref.at[start + shot // per_plane, pl.ds(lax.rem(shot, per_plane) * chunk, chunk)]
            for i in peers:
                peer = lax.rem(shot + i, shots)
                pltpu.make_async_remote_copy(
                    sums.at[h], dst, sum_send.at[h, i], sum_recv.at[h, i],
                    device_id={"shot": peer}, device_id_type=MESH,
                ).start()
            pltpu.make_async_copy(sums.at[h], dst, load_sem.at[h]).start()

        def reduce_drain(h, start):
            pltpu.make_async_copy(sums.at[h], out_ref.at[0, pl.ds(0, chunk)], load_sem.at[h]).wait()
            for i in peers:
                peer = lax.rem(shot + shots - i, shots)
                dst = out_ref.at[start + peer // per_plane, pl.ds(lax.rem(peer, per_plane) * chunk, chunk)]
                copy = pltpu.make_async_remote_copy(
                    sums.at[h], dst, sum_send.at[h, i], sum_recv.at[h, i],
                    device_id={"shot": peer}, device_id_type=MESH,
                )
                copy.wait_recv()
                copy.wait_send()
                pltpu.make_async_remote_copy(
                    parts.at[h, peer], parts.at[h, peer], part_send.at[h, i], part_recv.at[h, i],
                    device_id={"shot": peer}, device_id_type=MESH,
                ).wait_send()

        local(P_NOW)
        local(SQ_NOW)
        lax.fori_loop(0, depth, inject, 0)
        loads[4].wait()
        loads[5].wait()

        near_arrival(4).wait_recv()
        buoy_slope_z(inner)
        near_arrival(P_NOW).wait_recv()
        forward(False)
        near_copy(P_NEXT).start()
        near_arrival(SQ_NOW).wait_recv()
        backward(False)
        near_copy(SQ_NEXT).start()

        when_far(far_arrival(4).wait_recv)
        buoy_slope_z(outer)
        when_far(far_arrival(P_NOW).wait_recv)
        forward(True)
        when_far(far_copy(P_NEXT).start)
        when_far(far_arrival(SQ_NOW).wait_recv)
        backward(True)
        when_far(far_copy(SQ_NEXT).start)

        local(P_NEXT)
        local(SQ_NEXT)
        near_arrival(P_NEXT).wait_recv()
        near_arrival(SQ_NEXT).wait_recv()
        finish(False)
        reduce_start(0, inner)
        when_far(far_arrival(P_NEXT).wait_recv)
        when_far(far_arrival(SQ_NEXT).wait_recv)
        finish(True)
        reduce_start(1, outer)
        reduce_finish(0, inner)
        reduce_finish(1, outer)
        for f in range(5):
            when_far(far_copy(f).wait_send)
            near_copy(f).wait_send()
        reduce_drain(0, inner)
        reduce_drain(1, outer)

    return kernel


def solution(mesh):
    shots, doms = mesh.shape["shot"], mesh.shape["dom"]

    def shards(
        stiffness,
        buoyancy,
        forward_now,
        forward_prior,
        adjoint_now,
        adjoint_after,
        source_cells,
        wavelet,
        receiver_cells,
        residuals,
    ):
        depth, rows, lanes = stiffness.shape
        receivers = receiver_cells.shape[1]
        half = depth // 2
        chunk = half * rows // shots
        padded = (depth + 2 * WIDTH, rows + 2 * PAD, lanes)
        slab = (depth, rows, lanes)
        f32 = jnp.float32
        in_hbm = pl.BlockSpec(memory_space=pltpu.HBM)
        in_smem = pl.BlockSpec(memory_space=pltpu.SMEM)
        in_vmem = pl.BlockSpec(memory_space=pltpu.VMEM)
        return pl.pallas_call(
            make_kernel(shots, doms, depth, rows, lanes, receivers),
            out_shape=jax.ShapeDtypeStruct(slab, f32),
            in_specs=[in_hbm] * 6 + [in_smem] * 2 + [in_vmem] * 2,
            out_specs=in_hbm,
            scratch_shapes=[
                pltpu.VMEM(padded, f32),
                pltpu.VMEM((4, *padded), f32),
                pltpu.VMEM(slab, f32),
                pltpu.VMEM(slab, f32),
                pltpu.VMEM(slab, f32),
                pltpu.VMEM(slab, f32),
                pltpu.VMEM((4, half, rows, lanes), f32),
                pltpu.VMEM((4, half, rows, lanes), f32),
                pltpu.VMEM((3, *slab), f32),
                pltpu.VMEM((4, *slab), f32),
                pltpu.VMEM((4, *slab), f32),
                pltpu.VMEM(slab, f32),
                pltpu.VMEM(slab, f32),
                pltpu.VMEM((depth, rows, 2 * lanes), f32),
                pltpu.VMEM(slab, f32),
                pltpu.VMEM((2, shots, chunk, lanes), f32),
                pltpu.VMEM((2, chunk, lanes), f32),
                pltpu.SemaphoreType.DMA((6,)),
                pltpu.SemaphoreType.DMA((2, 5)),
                pltpu.SemaphoreType.DMA((2, 5)),
                pltpu.SemaphoreType.DMA((2, shots)),
                pltpu.SemaphoreType.DMA((2, shots)),
                pltpu.SemaphoreType.DMA((2, shots)),
                pltpu.SemaphoreType.DMA((2, shots)),
            ],
            compiler_params=pltpu.CompilerParams(
                collective_id=0, has_side_effects=True, vmem_limit_bytes=48 * 1024 * 1024
            ),
            name="window",
        )(
            stiffness, buoyancy, forward_now, forward_prior, adjoint_now, adjoint_after,
            source_cells, wavelet, receiver_cells, residuals,
        )

    placed = (
        P("dom", None, None),
        P("dom", None, None),
        P("shot", "dom", None, None),
        P("shot", "dom", None, None),
        P("shot", "dom", None, None),
        P("shot", "dom", None, None),
        P("shot"),
        P("shot", None),
        P("shot", None),
        P("shot", None, None),
    )
    return jax.shard_map(
        shards, mesh=mesh, in_specs=placed, out_specs=P("dom", None, None), check_vma=False
    )
```

```python
import jax
import jax.numpy as jnp
from jax import lax
from jax.experimental import pallas as pl
from jax.experimental.pallas import tpu as pltpu
from jax.sharding import PartitionSpec as P

C_SECOND = (-205.0 / 72.0, 8.0 / 5.0, -1.0 / 5.0, 8.0 / 315.0, -1.0 / 560.0)
C_FIRST = (4.0 / 5.0, -1.0 / 5.0, 4.0 / 105.0, -1.0 / 280.0)
MESH = pl.DeviceIdType.MESH
WIDTH = 4
P_NOW, SQ_NOW, P_NEXT, SQ_NEXT = range(4)


def make_kernel(shots, doms, depth, rows, lanes, receivers):
    plane = rows * lanes
    half = depth // 2
    length = shots // 2
    chunk = half * rows // shots
    wide = half * rows // length
    steps = sorted({1, length - 1})
    leaps = sorted({2 % length, (length - 2) % length} - {0})

    def kernel(
        stiff_hbm,
        buoy_hbm,
        now_hbm,
        prior_hbm,
        adj_hbm,
        after_hbm,
        source_ref,
        wavelet_ref,
        cells_ref,
        traces_ref,
        out_ref,
        buoy,
        fields,
        stiff,
        prior,
        adj,
        after,
        far_halo,
        near_halo,
        slopes,
        base,
        slope_z,
        image,
        adj_next,
        injected,
        left,
        right,
        grad,
        parts,
        sums,
        wide_parts,
        wide_sums,
        load_sem,
        halo_send,
        halo_recv,
        outer_send,
        outer_recv,
        inner_send,
        inner_recv,
        near_ready,
        greeted,
    ):
        shot = lax.axis_index("shot")
        dom = lax.axis_index("dom")
        core = lax.rem(dom, 2)
        near = dom + 1 - 2 * core
        far = dom - 1 + 2 * core
        has_far = (far >= 0) & (far < doms)
        far_count = jnp.where(has_far, 1, 0)
        outer = core * half
        inner = half - outer
        side = (2 * core - 1).astype(jnp.float32)

        row, column = shot // length, lax.rem(shot, length)

        def along(i):
            return {"shot": row * length + lax.rem(column + i, length)}

        across = {"shot": (1 - row) * length + column}
        peers = sorted(range(1, shots), key=lambda i: -min(i % length, length - i % length))
        line = sorted(range(1, length), key=lambda i: -min(i, length - i))

        barrier = pltpu.get_barrier_semaphore()

        @pl.when(has_far)
        def _():
            pl.semaphore_signal(barrier, 1, device_id={"dom": far}, device_id_type=MESH)

        @pl.when(core == 1)
        def _():
            pl.semaphore_signal(barrier, 1, device_id={"dom": near}, device_id_type=MESH)

        for i in steps:
            pl.semaphore_signal(barrier, 1, device_id=along(i), device_id_type=MESH)
        pl.semaphore_signal(barrier, 1, device_id=across, device_id_type=MESH)

        loads = [
            pltpu.make_async_copy(src, dst, load_sem.at[i])
            for i, (src, dst) in enumerate(
                (
                    (buoy_hbm, buoy.at[pl.ds(WIDTH, depth)]),
                    (now_hbm.at[0], fields.at[P_NOW, pl.ds(WIDTH, depth)]),
                    (stiff_hbm, stiff),
                    (adj_hbm.at[0], adj),
                    (prior_hbm.at[0], prior),
                    (after_hbm.at[0], after),
                )
            )
        ]
        for load in loads:
            load.start()

        blank = jnp.zeros((rows, lanes), jnp.float32)

        def clear(f, carry):
            for z in range(WIDTH):
                fields[f, z] = blank
                fields[f, WIDTH + depth + z] = blank
            return carry

        lax.fori_loop(0, 4, clear, 0)

        def split(value):
            high = value.astype(jnp.bfloat16)
            return high, (value - high.astype(jnp.float32)).astype(jnp.bfloat16)

        def second(offset):
            total = jnp.zeros(offset.shape, jnp.float32)
            for k in range(1, 5):
                total = jnp.where(jnp.abs(offset) == k, C_SECOND[k], total)
            return total

        def first(offset):
            total = jnp.zeros(offset.shape, jnp.float32)
            for k in range(1, 5):
                total = jnp.where(offset == k, C_FIRST[k - 1], total)
                total = jnp.where(offset == -k, -C_FIRST[k - 1], total)
            return total

        def first_extended(source, target, length):
            total = jnp.zeros(source.shape, jnp.float32)
            for k in range(1, 5):
                up = jnp.minimum(target + k, length - 1)
                down = jnp.maximum(target - k, 0)
                total = total + jnp.where(source == up, C_FIRST[k - 1], 0.0)
                total = total - jnp.where(source == down, C_FIRST[k - 1], 0.0)
            return total

        def make_matrices():
            source = lax.broadcasted_iota(jnp.int32, (lanes, lanes), 0)
            target = lax.broadcasted_iota(jnp.int32, (lanes, lanes), 1)
            offset = source - target
            centre = jnp.where(offset == 0, 3.0 * C_SECOND[0], 0.0)
            for at, value in enumerate(
                (second(offset) + centre, first(offset), first_extended(source, target, lanes))
            ):
                columns = pl.ds(at * lanes, lanes)
                high, low = split(value)
                right[0:lanes, columns] = high
                right[lanes : 2 * lanes, columns] = high
                right[2 * lanes : 3 * lanes, columns] = low
            target = lax.broadcasted_iota(jnp.int32, (rows, 3 * rows), 0)
            source = lax.rem(lax.broadcasted_iota(jnp.int32, (rows, 3 * rows), 1), rows)
            last = lax.broadcasted_iota(jnp.int32, (rows, 3 * rows), 1) >= 2 * rows
            offset = source - target
            for at, value in enumerate(
                (second(offset), first(offset), first_extended(source, target, rows))
            ):
                high, low = split(value)
                left[at * rows : (at + 1) * rows] = jnp.where(
                    last, low.astype(jnp.float32), high.astype(jnp.float32)
                ).astype(jnp.bfloat16)

        make_matrices()

        def dot(a, b):
            return lax.dot_general(
                a, b, (((1,), (0,)), ((), ())), preferred_element_type=jnp.float32
            )

        def differences(value, which):
            high, low = split(value)
            flat_high = high.reshape(2 * rows, lanes)
            flat = jnp.concatenate([flat_high, low.reshape(2 * rows, lanes)], axis=1)
            first_column, columns = (0, 2 * lanes) if which == 0 else (2 * lanes, lanes)
            use = pl.ds(first_column, columns)
            along_y = dot(flat, right[0 : 2 * lanes, use]) + dot(
                flat_high, right[2 * lanes : 3 * lanes, use]
            )
            stacked = jnp.concatenate(
                [jnp.concatenate([high[i], low[i], high[i]], axis=0) for i in range(2)], axis=1
            )
            use = pl.ds(0, 2 * rows) if which == 0 else pl.ds(2 * rows, rows)
            along_x = dot(left[use], stacked)
            return along_x, along_y

        loads[2].wait()
        loads[3].wait()

        def scale(z, carry):
            fields[SQ_NOW, WIDTH + z] = stiff[z] * adj[z]
            return carry

        lax.fori_loop(0, depth, scale, 0)
        loads[0].wait()
        loads[1].wait()

        def far_copy(f):
            if f == 4:
                src = buoy.at[pl.ds(WIDTH + outer, half)]
                dst = buoy.at[pl.ds((1 - core) * (WIDTH + depth), half)]
            else:
                src = fields.at[f, pl.ds(WIDTH + outer, half)]
                dst = far_halo.at[f]
            return pltpu.make_async_remote_copy(
                src, dst, halo_send.at[0, f], halo_recv.at[0, f], device_id={"dom": far}, device_id_type=MESH
            )

        def far_arrival(f):
            if f == 4:
                dst = buoy.at[pl.ds(core * (WIDTH + depth), half)]
            else:
                dst = far_halo.at[f]
            return pltpu.make_async_remote_copy(
                dst, dst, halo_send.at[0, f], halo_recv.at[0, f], device_id={"dom": far}, device_id_type=MESH
            )

        def near_copy(f):
            if f == 4:
                src = buoy.at[pl.ds(WIDTH + inner, half)]
                dst = buoy.at[pl.ds(core * (WIDTH + depth), half)]
            else:
                src = fields.at[f, pl.ds(WIDTH + inner, half)]
                dst = near_halo.at[f]
            return pltpu.make_async_remote_copy(
                src, dst, halo_send.at[1, f], halo_recv.at[1, f], device_id={"dom": near}, device_id_type=MESH
            )

        def near_arrival(f):
            if f == 4:
                dst = buoy.at[pl.ds((1 - core) * (WIDTH + depth), half)]
            else:
                dst = near_halo.at[f]
            return pltpu.make_async_remote_copy(
                dst, dst, halo_send.at[1, f], halo_recv.at[1, f], device_id={"dom": near}, device_id_type=MESH
            )

        def when_far(act):
            pl.when(has_far)(act)

        def buoy_slopes():
            for z in range(0, depth, 2):
                along_x, along_y = differences(buoy[WIDTH + z : WIDTH + z + 2], 1)
                for i in range(2):
                    slopes[0, z + i] = along_x[:, i * lanes : (i + 1) * lanes]
                    slopes[1, z + i] = along_y[i * rows : (i + 1) * rows]

        def buoy_slope_z(start):
            def body(j, carry):
                z = start + j
                along_z = jnp.zeros((rows, lanes), jnp.float32)
                for k in range(1, 5):
                    up = buoy[WIDTH + z + k]
                    down = buoy[WIDTH + z - k]
                    along_z = along_z + C_FIRST[k - 1] * (up - down)
                slopes[2, z] = along_z
                return carry

            lax.fori_loop(0, half, body, 0)

        def local(f):
            for z0 in range(0, depth, 2):
                along_x, along_y = differences(fields[f, WIDTH + z0 : WIDTH + z0 + 2], 0)
                for i in range(2):
                    z = z0 + i
                    of_x = slice(i * lanes, (i + 1) * lanes)
                    of_y = slice(i * rows, (i + 1) * rows)
                    curve = along_x[0:rows, of_x] + along_y[of_y, 0:lanes]
                    along = jnp.zeros((rows, lanes), jnp.float32)
                    for k in range(1, 5):
                        up = fields[f, WIDTH + z + k]
                        down = fields[f, WIDTH + z - k]
                        curve = curve + C_SECOND[k] * (up + down)
                        along = along + C_FIRST[k - 1] * (up - down)
                    slope_z[f, z] = along
                    base[f, z] = (
                        buoy[WIDTH + z] * curve
                        + along_x[rows : 2 * rows, of_x] * slopes[0, z]
                        + along_y[of_y, lanes : 2 * lanes] * slopes[1, z]
                    )

        buoy_slopes()
        local(P_NOW)
        local(SQ_NOW)
        pl.semaphore_wait(barrier, len(steps) + 1 + far_count + (1 - core))

        for f in (4, P_NOW, SQ_NOW):
            when_far(far_copy(f).start)

        def near_begin():
            @pl.when(core == 0)
            def _():
                pl.semaphore_signal(near_ready, 1, device_id={"dom": near}, device_id_type=MESH)

            @pl.when(core == 1)
            def _():
                pl.semaphore_wait(near_ready, 1)

            for f in (4, P_NOW, SQ_NOW):
                near_copy(f).start()

        pl.when(dom != 1)(near_begin)
        for i in steps:
            pl.semaphore_signal(greeted.at[0], 1, device_id=along(i), device_id_type=MESH)

        @pl.when(jnp.logical_not(has_far))
        def _():
            edge = buoy[WIDTH + core * (depth - 1)]
            for z in range(half):
                buoy[core * (WIDTH + depth) + z] = edge
                for f in range(4):
                    far_halo[f, z] = blank

        def whole(f, j, is_far):
            halo = far_halo if is_far else near_halo
            up = core if is_far else 1 - core
            z = up * (depth - 1 - j) + (1 - up) * j
            curve = jnp.zeros((rows, lanes), jnp.float32)
            along = jnp.zeros((rows, lanes), jnp.float32)
            for k in range(j + 1, 5):
                m = k - j
                plane_at = up * (m - 1) + (1 - up) * (half - m)
                value = halo[f, plane_at]
                curve = curve + C_SECOND[k] * value
                along = along + C_FIRST[k - 1] * value
            sign = side if is_far else -side
            along = slope_z[f, z] + sign * along
            return z, base[f, z] + buoy[WIDTH + z] * curve + along * slopes[2, z]

        for load in loads[4:]:
            load.wait()
        local_source = source_ref[...].reshape(1, 1) - dom * (depth * plane)
        amplitude = wavelet_ref[...]
        cell = lax.broadcasted_iota(jnp.int32, (rows, lanes), 0) * lanes
        cell = cell + lax.broadcasted_iota(jnp.int32, (rows, lanes), 1)

        def forward(is_far):
            for j in range(half):
                z, value = whole(P_NOW, j, is_far)
                image[z] = value
                shown = jnp.where(cell + z * plane == local_source, amplitude, 0.0)
                fields[P_NEXT, WIDTH + z] = (
                    2.0 * fields[P_NOW, WIDTH + z] - prior[z] + stiff[z] * value + shown
                )

        def backward(is_far):
            for j in range(half):
                z, value = whole(SQ_NOW, j, is_far)
                value = 2.0 * adj[z] - after[z] + value + injected[pl.ds(z * rows, rows), 0:lanes]
                adj_next[z] = value
                fields[SQ_NEXT, WIDTH + z] = stiff[z] * value

        def finish(is_far):
            for j in range(half):
                z, last_image = whole(P_NEXT, j, is_far)
                _, value = whole(SQ_NEXT, j, is_far)
                newer = adj_next[z]
                value = 2.0 * newer - adj[z] + value + injected[pl.ds(z * rows, rows), lanes : 2 * lanes]
                grad[pl.ds(z * rows, rows)] = newer * last_image + value * image[z]

        def inject():
            local_cells = cells_ref[...] - dom * (depth * plane)
            cell_rows = jnp.right_shift(local_cells, 7)
            cell_lanes = jnp.bitwise_and(local_cells, lanes - 1)
            lane_hot = lax.broadcasted_iota(jnp.int32, (lanes, receivers), 0) == cell_lanes
            amounts = jnp.concatenate(
                [jnp.where(lane_hot, traces_ref[0, k : k + 1, :], 0.0) for k in range(2)], axis=0
            )
            amounts = amounts.T
            high, _ = split(amounts)
            middle, low = split(amounts - high.astype(jnp.float32))
            row = lax.broadcasted_iota(jnp.int32, (depth * rows, receivers), 0)
            row_hot = jnp.where(row == cell_rows, 1.0, 0.0).astype(jnp.bfloat16)
            injected[...] = dot(row_hot, low) + dot(row_hot, middle) + dot(row_hot, high)

        def share(of):
            return pl.ds(outer * rows + of * chunk, chunk)

        def outer_copy(stage, i):
            peer = lax.rem(shot + i, shots)
            if stage == 0:
                src, dst = grad.at[share(peer)], parts.at[shot]
            else:
                src, dst = sums, out_ref.at[share(shot)]
            return pltpu.make_async_remote_copy(
                src, dst, outer_send.at[stage], outer_recv.at[stage], device_id={"shot": peer}, device_id_type=MESH
            )

        def outer_all(stage):
            every = parts.at[pl.ds(0, shots - 1)]
            return pltpu.make_async_remote_copy(
                every, every, outer_send.at[stage], outer_recv.at[stage], device_id=across, device_id_type=MESH
            )

        def wide_share(of):
            return pl.ds(inner * rows + of * wide, wide)

        def inner_copy(stage, i):
            peer = lax.rem(column + i, length)
            if stage == 0:
                src, dst = grad.at[wide_share(peer)], wide_parts.at[column]
            else:
                src, dst = wide_sums.at[2], out_ref.at[wide_share(column)]
            return pltpu.make_async_remote_copy(
                src, dst, inner_send.at[stage], inner_recv.at[stage], device_id=along(i), device_id_type=MESH
            )

        def inner_all(stage):
            every = wide_parts.at[pl.ds(0, length - 1)]
            return pltpu.make_async_remote_copy(
                every, every, inner_send.at[stage], inner_recv.at[stage], device_id=across, device_id_type=MESH
            )

        swap = pltpu.make_async_remote_copy(
            wide_sums.at[0], wide_sums.at[1], inner_send.at[2], inner_recv.at[2], device_id=across, device_id_type=MESH
        )

        def near_fold():
            near_arrival(4).wait_recv()
            buoy_slope_z(inner)
            near_arrival(P_NOW).wait_recv()
            forward(False)
            near_copy(P_NEXT).start()
            near_arrival(SQ_NOW).wait_recv()
            backward(False)
            near_copy(SQ_NEXT).start()

        inject()

        when_far(far_arrival(4).wait_recv)
        buoy_slope_z(outer)
        when_far(far_arrival(P_NOW).wait_recv)
        forward(True)
        when_far(far_copy(P_NEXT).start)

        pl.semaphore_wait(greeted.at[0], len(steps))
        for i in leaps:
            pl.semaphore_signal(greeted.at[1], 1, device_id=along(i), device_id_type=MESH)
        pl.when(dom != 1)(near_fold)

        when_far(far_arrival(SQ_NOW).wait_recv)
        backward(True)
        when_far(far_copy(SQ_NEXT).start)

        @pl.when(dom == 1)
        def _():
            near_begin()
            near_fold()

        if leaps:
            pl.semaphore_wait(greeted.at[1], len(leaps))
        pl.semaphore_signal(greeted.at[2], 1, device_id=across, device_id_type=MESH)

        local(P_NEXT)
        local(SQ_NEXT)
        near_arrival(P_NEXT).wait_recv()
        near_arrival(SQ_NEXT).wait_recv()
        finish(False)
        for i in line:
            inner_copy(0, i).start()
        pl.semaphore_wait(greeted.at[2], 1)

        when_far(far_arrival(P_NEXT).wait_recv)
        when_far(far_arrival(SQ_NEXT).wait_recv)
        finish(True)
        for i in peers:
            outer_copy(0, i).start()

        inner_all(0).wait_recv()
        total = grad[wide_share(column)]
        for i in line:
            total = total + wide_parts[lax.rem(column + i, length)]
        wide_sums[0] = total
        swap.start()
        swap.wait_recv()
        wide_sums[2] = wide_sums[0] + wide_sums[1]
        for i in line:
            inner_copy(1, i).start()
        out_ref[wide_share(column)] = wide_sums[2]

        outer_all(0).wait_recv()
        total = grad[share(shot)]
        for i in peers:
            total = total + parts[lax.rem(shot + i, shots)]
        sums[...] = total
        for i in peers:
            outer_copy(1, i).start()
        out_ref[share(shot)] = total

        for f in range(5):
            when_far(far_copy(f).wait_send)
            near_copy(f).wait_send()
        swap.wait_send()
        for stage in range(2):
            inner_all(stage).wait_send()
        outer_all(0).wait_send()
        inner_all(1).wait_recv()
        outer_all(1).wait_send()
        outer_all(1).wait_recv()

    return kernel


def solution(mesh):
    shots, doms = mesh.shape["shot"], mesh.shape["dom"]

    def shards(
        stiffness,
        buoyancy,
        forward_now,
        forward_prior,
        adjoint_now,
        adjoint_after,
        source_cells,
        wavelet,
        receiver_cells,
        residuals,
    ):
        depth, rows, lanes = stiffness.shape
        receivers = receiver_cells.shape[1]
        half = depth // 2
        length = shots // 2
        chunk = half * rows // shots
        wide = half * rows // length
        padded = (depth + 2 * WIDTH, rows, lanes)
        slab = (depth, rows, lanes)
        f32 = jnp.float32
        in_hbm = pl.BlockSpec(memory_space=pltpu.HBM)
        return pl.pallas_call(
            make_kernel(shots, doms, depth, rows, lanes, receivers),
            out_shape=jax.ShapeDtypeStruct((depth * rows, lanes), f32),
            in_specs=[in_hbm] * 6 + [pl.BlockSpec(memory_space=pltpu.VMEM)] * 4,
            out_specs=pl.BlockSpec(memory_space=pltpu.VMEM),
            scratch_shapes=[
                pltpu.VMEM(padded, f32),
                pltpu.VMEM((4, *padded), f32),
                pltpu.VMEM(slab, f32),
                pltpu.VMEM(slab, f32),
                pltpu.VMEM(slab, f32),
                pltpu.VMEM(slab, f32),
                pltpu.VMEM((4, half, rows, lanes), f32),
                pltpu.VMEM((4, half, rows, lanes), f32),
                pltpu.VMEM((3, *slab), f32),
                pltpu.VMEM((4, *slab), f32),
                pltpu.VMEM((4, *slab), f32),
                pltpu.VMEM(slab, f32),
                pltpu.VMEM(slab, f32),
                pltpu.VMEM((depth * rows, 2 * lanes), f32),
                pltpu.VMEM((3 * rows, 3 * rows), jnp.bfloat16),
                pltpu.VMEM((3 * lanes, 3 * lanes), jnp.bfloat16),
                pltpu.VMEM((depth * rows, lanes), f32),
                pltpu.VMEM((shots, chunk, lanes), f32),
                pltpu.VMEM((chunk, lanes), f32),
                pltpu.VMEM((length, wide, lanes), f32),
                pltpu.VMEM((3, wide, lanes), f32),
                pltpu.SemaphoreType.DMA((6,)),
                pltpu.SemaphoreType.DMA((2, 5)),
                pltpu.SemaphoreType.DMA((2, 5)),
                pltpu.SemaphoreType.DMA((2,)),
                pltpu.SemaphoreType.DMA((2,)),
                pltpu.SemaphoreType.DMA((3,)),
                pltpu.SemaphoreType.DMA((3,)),
                pltpu.SemaphoreType.REGULAR,
                pltpu.SemaphoreType.REGULAR((3,)),
            ],
            compiler_params=pltpu.CompilerParams(
                collective_id=0, has_side_effects=True, vmem_limit_bytes=54800 * 1024
            ),
            name="window",
        )(
            stiffness, buoyancy, forward_now, forward_prior, adjoint_now, adjoint_after,
            source_cells, wavelet, receiver_cells, residuals,
        ).reshape(slab)

    placed = (
        P("dom", None, None),
        P("dom", None, None),
        P("shot", "dom", None, None),
        P("shot", "dom", None, None),
        P("shot", "dom", None, None),
        P("shot", "dom", None, None),
        P("shot"),
        P("shot", None),
        P("shot", None),
        P("shot", None, None),
    )
    return jax.shard_map(
        shards, mesh=mesh, in_specs=placed, out_specs=P("dom", None, None), check_vma=False
    )
```

```python
import jax
import jax.numpy as jnp
from jax import lax
from jax.experimental import pallas as pl
from jax.experimental.pallas import tpu as pltpu
from jax.sharding import PartitionSpec as P

C_SECOND = (-205.0 / 72.0, 8.0 / 5.0, -1.0 / 5.0, 8.0 / 315.0, -1.0 / 560.0)
C_FIRST = (4.0 / 5.0, -1.0 / 5.0, 4.0 / 105.0, -1.0 / 280.0)
MESH = pl.DeviceIdType.MESH
WIDTH = 4
P_NOW, SQ_NOW, P_NEXT, SQ_NEXT = range(4)


def make_kernel(shots, doms, depth, rows, lanes, receivers):
    plane = rows * lanes
    half = depth // 2
    length = shots // 2
    chunk = half * rows // shots
    wide = half * rows // length
    band = rows // 2
    steps = sorted({1, length - 1})
    leaps = sorted({2 % length, (length - 2) % length} - {0})

    def kernel(
        stiff_hbm,
        buoy_hbm,
        now_hbm,
        prior_hbm,
        adj_hbm,
        after_hbm,
        source_ref,
        wavelet_ref,
        cells_ref,
        traces_ref,
        out_ref,
        buoy,
        fields,
        stiff,
        prior,
        adj,
        after,
        far_halo,
        near_halo,
        slopes,
        base,
        slope_z,
        image,
        adj_next,
        injected,
        left,
        right,
        grad,
        parts,
        sums,
        wide_parts,
        wide_sums,
        load_sem,
        far_send,
        far_recv,
        near_send,
        near_recv,
        outer_send,
        outer_recv,
        inner_send,
        inner_recv,
        near_ready,
        greeted,
    ):
        shot = lax.axis_index("shot")
        dom = lax.axis_index("dom")
        core = lax.rem(dom, 2)
        near = dom + 1 - 2 * core
        far = dom - 1 + 2 * core
        has_far = (far >= 0) & (far < doms)
        far_count = jnp.where(has_far, 1, 0)
        outer = core * half
        inner = half - outer
        side = (2 * core - 1).astype(jnp.float32)

        row, column = shot // length, lax.rem(shot, length)

        def along(i):
            return {"shot": row * length + lax.rem(column + i, length)}

        across = {"shot": (1 - row) * length + column}
        peers = sorted(range(1, shots), key=lambda i: -min(i % length, length - i % length))
        line = sorted(range(1, length), key=lambda i: -min(i, length - i))

        barrier = pltpu.get_barrier_semaphore()

        @pl.when(has_far)
        def _():
            pl.semaphore_signal(barrier, 1, device_id={"dom": far}, device_id_type=MESH)

        @pl.when(core == 1)
        def _():
            pl.semaphore_signal(barrier, 1, device_id={"dom": near}, device_id_type=MESH)

        for i in steps:
            pl.semaphore_signal(barrier, 1, device_id=along(i), device_id_type=MESH)
        pl.semaphore_signal(barrier, 1, device_id=across, device_id_type=MESH)

        loads = [
            pltpu.make_async_copy(src, dst, load_sem.at[i])
            for i, (src, dst) in enumerate(
                (
                    (buoy_hbm, buoy.at[pl.ds(WIDTH, depth)]),
                    (now_hbm.at[0], fields.at[P_NOW, pl.ds(WIDTH, depth)]),
                    (stiff_hbm, stiff),
                    (adj_hbm.at[0], adj),
                    (prior_hbm.at[0], prior),
                    (after_hbm.at[0], after),
                )
            )
        ]
        for load in loads:
            load.start()

        blank = jnp.zeros((rows, lanes), jnp.float32)

        def clear(f, carry):
            for z in range(WIDTH):
                fields[f, z] = blank
                fields[f, WIDTH + depth + z] = blank
            return carry

        lax.fori_loop(0, 4, clear, 0)

        def split(value):
            high = value.astype(jnp.bfloat16)
            return high, (value - high.astype(jnp.float32)).astype(jnp.bfloat16)

        def second(offset):
            total = jnp.zeros(offset.shape, jnp.float32)
            for k in range(1, 5):
                total = jnp.where(jnp.abs(offset) == k, C_SECOND[k], total)
            return total

        def first(offset):
            total = jnp.zeros(offset.shape, jnp.float32)
            for k in range(1, 5):
                total = jnp.where(offset == k, C_FIRST[k - 1], total)
                total = jnp.where(offset == -k, -C_FIRST[k - 1], total)
            return total

        def first_extended(source, target, length):
            total = jnp.zeros(source.shape, jnp.float32)
            for k in range(1, 5):
                up = jnp.minimum(target + k, length - 1)
                down = jnp.maximum(target - k, 0)
                total = total + jnp.where(source == up, C_FIRST[k - 1], 0.0)
                total = total - jnp.where(source == down, C_FIRST[k - 1], 0.0)
            return total

        def make_matrices():
            source = lax.broadcasted_iota(jnp.int32, (lanes, lanes), 0)
            target = lax.broadcasted_iota(jnp.int32, (lanes, lanes), 1)
            offset = source - target
            centre = jnp.where(offset == 0, 3.0 * C_SECOND[0], 0.0)
            for at, value in enumerate(
                (second(offset) + centre, first(offset), first_extended(source, target, lanes))
            ):
                columns = pl.ds(at * lanes, lanes)
                high, low = split(value)
                right[0:lanes, columns] = high
                right[lanes : 2 * lanes, columns] = high
                right[2 * lanes : 3 * lanes, columns] = low
            target = lax.broadcasted_iota(jnp.int32, (rows, 3 * rows), 0)
            source = lax.rem(lax.broadcasted_iota(jnp.int32, (rows, 3 * rows), 1), rows)
            last = lax.broadcasted_iota(jnp.int32, (rows, 3 * rows), 1) >= 2 * rows
            offset = source - target
            for at, value in enumerate(
                (second(offset), first(offset), first_extended(source, target, rows))
            ):
                high, low = split(value)
                left[at * rows : (at + 1) * rows] = jnp.where(
                    last, low.astype(jnp.float32), high.astype(jnp.float32)
                ).astype(jnp.bfloat16)

        def dot(a, b):
            return lax.dot_general(
                a, b, (((1,), (0,)), ((), ())), preferred_element_type=jnp.float32
            )

        def differences(value, which):
            high, low = split(value)
            flat_high = high.reshape(2 * rows, lanes)
            flat = jnp.concatenate([flat_high, low.reshape(2 * rows, lanes)], axis=1)
            first_column, columns = (0, 2 * lanes) if which == 0 else (2 * lanes, lanes)
            use = pl.ds(first_column, columns)
            along_y = dot(flat, right[0 : 2 * lanes, use]) + dot(
                flat_high, right[2 * lanes : 3 * lanes, use]
            )
            stacked = jnp.concatenate(
                [jnp.concatenate([high[i], low[i], high[i]], axis=0) for i in range(2)], axis=1
            )
            use = pl.ds(0, 2 * rows) if which == 0 else pl.ds(2 * rows, rows)
            along_x = dot(left[use], stacked)
            return along_x, along_y

        def scale(z, carry):
            fields[SQ_NOW, WIDTH + z] = stiff[z] * adj[z]
            return carry

        def far_ends(f, part, sending):
            of = pl.ds(part * band, band)
            if f < 4:
                return far_halo.at[f, pl.ds(0, half), of]
            at = 1 - core if sending else core
            return buoy.at[pl.ds(at * (WIDTH + depth), half), of]

        def far_copy(f, part):
            src = (buoy if f == 4 else fields.at[f]).at[pl.ds(WIDTH + outer, half), pl.ds(part * band, band)]
            return pltpu.make_async_remote_copy(
                src, far_ends(f, part, True), far_send.at[f, part], far_recv.at[f, part],
                device_id={"dom": far}, device_id_type=MESH,
            )

        def far_arrival(f, part):
            dst = far_ends(f, part, False)
            return pltpu.make_async_remote_copy(
                dst, dst, far_send.at[f, part], far_recv.at[f, part],
                device_id={"dom": far}, device_id_type=MESH,
            )

        def near_copy(f):
            if f == 4:
                src = buoy.at[pl.ds(WIDTH + inner, half)]
                dst = buoy.at[pl.ds(core * (WIDTH + depth), half)]
            else:
                src = fields.at[f, pl.ds(WIDTH + inner, half)]
                dst = near_halo.at[f]
            return pltpu.make_async_remote_copy(
                src, dst, near_send.at[f], near_recv.at[f], device_id={"dom": near}, device_id_type=MESH
            )

        def near_arrival(f):
            if f == 4:
                dst = buoy.at[pl.ds((1 - core) * (WIDTH + depth), half)]
            else:
                dst = near_halo.at[f]
            return pltpu.make_async_remote_copy(
                dst, dst, near_send.at[f], near_recv.at[f], device_id={"dom": near}, device_id_type=MESH
            )

        def when_far(act):
            pl.when(has_far)(act)

        def buoy_slopes():
            for z in range(0, depth, 2):
                along_x, along_y = differences(buoy[WIDTH + z : WIDTH + z + 2], 1)
                for i in range(2):
                    slopes[0, z + i] = along_x[:, i * lanes : (i + 1) * lanes]
                    slopes[1, z + i] = along_y[i * rows : (i + 1) * rows]

        def buoy_slope_z(start, use):
            def body(j, carry):
                z = start + j
                along_z = jnp.zeros((use.size, lanes), jnp.float32)
                for k in range(1, 5):
                    up = buoy[WIDTH + z + k, use]
                    down = buoy[WIDTH + z - k, use]
                    along_z = along_z + C_FIRST[k - 1] * (up - down)
                slopes[2, z, use] = along_z
                return carry

            lax.fori_loop(0, half, body, 0)

        def local(f):
            for z0 in range(0, depth, 2):
                along_x, along_y = differences(fields[f, WIDTH + z0 : WIDTH + z0 + 2], 0)
                for i in range(2):
                    z = z0 + i
                    of_x = slice(i * lanes, (i + 1) * lanes)
                    of_y = slice(i * rows, (i + 1) * rows)
                    curve = along_x[0:rows, of_x] + along_y[of_y, 0:lanes]
                    along = jnp.zeros((rows, lanes), jnp.float32)
                    for k in range(1, 5):
                        up = fields[f, WIDTH + z + k]
                        down = fields[f, WIDTH + z - k]
                        curve = curve + C_SECOND[k] * (up + down)
                        along = along + C_FIRST[k - 1] * (up - down)
                    slope_z[f, z] = along
                    base[f, z] = (
                        buoy[WIDTH + z] * curve
                        + along_x[rows : 2 * rows, of_x] * slopes[0, z]
                        + along_y[of_y, lanes : 2 * lanes] * slopes[1, z]
                    )

        loads[0].wait()
        loads[1].wait()
        pl.semaphore_wait(barrier, len(steps) + 1 + far_count + (1 - core))

        for part in range(2):
            for f in (4, P_NOW):
                when_far(far_copy(f, part).start)
        loads[2].wait()
        loads[3].wait()
        lax.fori_loop(0, depth, scale, 0)
        for part in range(2):
            when_far(far_copy(SQ_NOW, part).start)

        def near_begin():
            @pl.when(core == 0)
            def _():
                pl.semaphore_signal(near_ready, 1, device_id={"dom": near}, device_id_type=MESH)

            @pl.when(core == 1)
            def _():
                pl.semaphore_wait(near_ready, 1)

            for f in (4, P_NOW, SQ_NOW):
                near_copy(f).start()

        pl.when(dom != 1)(near_begin)
        for i in steps:
            pl.semaphore_signal(greeted.at[0], 1, device_id=along(i), device_id_type=MESH)

        make_matrices()
        buoy_slopes()
        local(P_NOW)
        local(SQ_NOW)

        @pl.when(jnp.logical_not(has_far))
        def _():
            edge = buoy[WIDTH + core * (depth - 1)]
            for z in range(half):
                buoy[core * (WIDTH + depth) + z] = edge
                for f in range(4):
                    far_halo[f, z] = blank

        def whole(f, j, is_far, use):
            halo = far_halo if is_far else near_halo
            up = core if is_far else 1 - core
            z = up * (depth - 1 - j) + (1 - up) * j
            curve = jnp.zeros((use.size, lanes), jnp.float32)
            along = jnp.zeros((use.size, lanes), jnp.float32)
            for k in range(j + 1, 5):
                m = k - j
                plane_at = up * (m - 1) + (1 - up) * (half - m)
                value = halo[f, plane_at, use]
                curve = curve + C_SECOND[k] * value
                along = along + C_FIRST[k - 1] * value
            sign = side if is_far else -side
            along = slope_z[f, z, use] + sign * along
            value = base[f, z, use] + buoy[WIDTH + z, use] * curve + along * slopes[2, z, use]
            return z, value

        for load in loads[4:]:
            load.wait()
        local_source = source_ref[...].reshape(1, 1) - dom * (depth * plane)
        amplitude = wavelet_ref[...]
        everything = pl.ds(0, rows)

        def forward(is_far, use=everything):
            cell = lax.broadcasted_iota(jnp.int32, (use.size, lanes), 0) * lanes
            cell = cell + lax.broadcasted_iota(jnp.int32, (use.size, lanes), 1)
            for j in range(half):
                z, value = whole(P_NOW, j, is_far, use)
                image[z, use] = value
                here = cell + (z * plane + use.start * lanes)
                shown = jnp.where(here == local_source, amplitude, 0.0)
                fields[P_NEXT, WIDTH + z, use] = (
                    2.0 * fields[P_NOW, WIDTH + z, use] - prior[z, use] + stiff[z, use] * value + shown
                )

        def backward(is_far, use=everything):
            for j in range(half):
                z, value = whole(SQ_NOW, j, is_far, use)
                injected_rows = pl.ds(z * rows + use.start, use.size)
                value = 2.0 * adj[z, use] - after[z, use] + value + injected[injected_rows, 0:lanes]
                adj_next[z, use] = value
                fields[SQ_NEXT, WIDTH + z, use] = stiff[z, use] * value

        def finish(is_far, use=everything):
            for j in range(half):
                z, last_image = whole(P_NEXT, j, is_far, use)
                _, value = whole(SQ_NEXT, j, is_far, use)
                newer = adj_next[z, use]
                flat = pl.ds(z * rows + use.start, use.size)
                value = 2.0 * newer - adj[z, use] + value + injected[flat, lanes : 2 * lanes]
                grad[flat] = newer * last_image + value * image[z, use]

        def inject():
            local_cells = cells_ref[...] - dom * (depth * plane)
            cell_rows = jnp.right_shift(local_cells, 7)
            cell_lanes = jnp.bitwise_and(local_cells, lanes - 1)
            lane_hot = lax.broadcasted_iota(jnp.int32, (lanes, receivers), 0) == cell_lanes
            amounts = jnp.concatenate(
                [jnp.where(lane_hot, traces_ref[0, k : k + 1, :], 0.0) for k in range(2)], axis=0
            )
            amounts = amounts.T
            high, _ = split(amounts)
            middle, low = split(amounts - high.astype(jnp.float32))
            row = lax.broadcasted_iota(jnp.int32, (depth * rows, receivers), 0)
            row_hot = jnp.where(row == cell_rows, 1.0, 0.0).astype(jnp.bfloat16)
            injected[...] = dot(row_hot, low) + dot(row_hot, middle) + dot(row_hot, high)

        def share(of_row, of_column):
            at = of_column * chunk
            return pl.ds((outer + at // band) * rows + of_row * band + lax.rem(at, band), chunk)

        def outer_copy(stage, to_row, i):
            to_column = lax.rem(column + i, length)
            if stage == 0:
                src, dst = grad.at[share(to_row, to_column)], parts.at[shot]
            else:
                src, dst = sums, out_ref.at[share(row, column)]
            return pltpu.make_async_remote_copy(
                src, dst, outer_send.at[stage], outer_recv.at[stage],
                device_id={"shot": to_row * length + to_column}, device_id_type=MESH,
            )

        def outer_start(stage, to_row):
            for i in line:
                outer_copy(stage, to_row, i).start()
            pl.when(row != to_row)(outer_copy(stage, to_row, 0).start)

        def outer_all(stage):
            every = parts.at[pl.ds(0, shots - 1)]
            return pltpu.make_async_remote_copy(
                every, every, outer_send.at[stage], outer_recv.at[stage], device_id=across, device_id_type=MESH
            )

        def wide_share(of):
            return pl.ds(inner * rows + of * wide, wide)

        def inner_copy(stage, i):
            peer = lax.rem(column + i, length)
            if stage == 0:
                src, dst = grad.at[wide_share(peer)], wide_parts.at[column]
            else:
                src, dst = wide_sums.at[2], out_ref.at[wide_share(column)]
            return pltpu.make_async_remote_copy(
                src, dst, inner_send.at[stage], inner_recv.at[stage], device_id=along(i), device_id_type=MESH
            )

        def inner_all(stage):
            every = wide_parts.at[pl.ds(0, length - 1)]
            return pltpu.make_async_remote_copy(
                every, every, inner_send.at[stage], inner_recv.at[stage], device_id=across, device_id_type=MESH
            )

        swap = pltpu.make_async_remote_copy(
            wide_sums.at[0], wide_sums.at[1], inner_send.at[2], inner_recv.at[2], device_id=across, device_id_type=MESH
        )

        def near_fold():
            near_arrival(4).wait_recv()
            buoy_slope_z(inner, everything)
            near_arrival(P_NOW).wait_recv()
            forward(False)
            near_copy(P_NEXT).start()
            near_arrival(SQ_NOW).wait_recv()
            backward(False)
            near_copy(SQ_NEXT).start()

        inject()

        for part in range(2):
            use = pl.ds(part * band, band)
            when_far(far_arrival(4, part).wait_recv)
            buoy_slope_z(outer, use)
            when_far(far_arrival(P_NOW, part).wait_recv)
            forward(True, use)
            when_far(far_copy(P_NEXT, part).start)

        pl.semaphore_wait(greeted.at[0], len(steps))
        for i in leaps:
            pl.semaphore_signal(greeted.at[1], 1, device_id=along(i), device_id_type=MESH)
        pl.when(dom != 1)(near_fold)

        for part in range(2):
            when_far(far_arrival(SQ_NOW, part).wait_recv)
            backward(True, pl.ds(part * band, band))
            when_far(far_copy(SQ_NEXT, part).start)

        @pl.when(dom == 1)
        def _():
            near_begin()
            near_fold()

        if leaps:
            pl.semaphore_wait(greeted.at[1], len(leaps))
        pl.semaphore_signal(greeted.at[2], 1, device_id=across, device_id_type=MESH)

        local(P_NEXT)
        local(SQ_NEXT)
        near_arrival(P_NEXT).wait_recv()
        near_arrival(SQ_NEXT).wait_recv()
        finish(False)
        for i in line:
            inner_copy(0, i).start()
        pl.semaphore_wait(greeted.at[2], 1)

        for part in range(2):
            when_far(far_arrival(P_NEXT, part).wait_recv)
            when_far(far_arrival(SQ_NEXT, part).wait_recv)
            finish(True, pl.ds(part * band, band))
            outer_start(0, part)

        inner_all(0).wait_recv()
        total = grad[wide_share(column)]
        for i in line:
            total = total + wide_parts[lax.rem(column + i, length)]
        wide_sums[0] = total
        swap.start()
        swap.wait_recv()
        wide_sums[2] = wide_sums[0] + wide_sums[1]
        for i in line:
            inner_copy(1, i).start()
        out_ref[wide_share(column)] = wide_sums[2]

        outer_all(0).wait_recv()
        total = grad[share(row, column)]
        for i in peers:
            total = total + parts[lax.rem(shot + i, shots)]
        sums[...] = total
        for to_row in range(2):
            outer_start(1, to_row)
        out_ref[share(row, column)] = total

        for f in range(5):
            for part in range(2):
                when_far(far_copy(f, part).wait_send)
            near_copy(f).wait_send()
        swap.wait_send()
        for stage in range(2):
            inner_all(stage).wait_send()
        outer_all(0).wait_send()
        inner_all(1).wait_recv()
        outer_all(1).wait_send()
        outer_all(1).wait_recv()

    return kernel


def solution(mesh):
    shots, doms = mesh.shape["shot"], mesh.shape["dom"]

    def shards(
        stiffness,
        buoyancy,
        forward_now,
        forward_prior,
        adjoint_now,
        adjoint_after,
        source_cells,
        wavelet,
        receiver_cells,
        residuals,
    ):
        depth, rows, lanes = stiffness.shape
        receivers = receiver_cells.shape[1]
        half = depth // 2
        length = shots // 2
        chunk = half * rows // shots
        wide = half * rows // length
        padded = (depth + 2 * WIDTH, rows, lanes)
        slab = (depth, rows, lanes)
        f32 = jnp.float32
        in_hbm = pl.BlockSpec(memory_space=pltpu.HBM)
        return pl.pallas_call(
            make_kernel(shots, doms, depth, rows, lanes, receivers),
            out_shape=jax.ShapeDtypeStruct((depth * rows, lanes), f32),
            in_specs=[in_hbm] * 6 + [pl.BlockSpec(memory_space=pltpu.VMEM)] * 4,
            out_specs=pl.BlockSpec(memory_space=pltpu.VMEM),
            scratch_shapes=[
                pltpu.VMEM(padded, f32),
                pltpu.VMEM((4, *padded), f32),
                pltpu.VMEM(slab, f32),
                pltpu.VMEM(slab, f32),
                pltpu.VMEM(slab, f32),
                pltpu.VMEM(slab, f32),
                pltpu.VMEM((4, half, rows, lanes), f32),
                pltpu.VMEM((4, half, rows, lanes), f32),
                pltpu.VMEM((3, *slab), f32),
                pltpu.VMEM((4, *slab), f32),
                pltpu.VMEM((4, *slab), f32),
                pltpu.VMEM(slab, f32),
                pltpu.VMEM(slab, f32),
                pltpu.VMEM((depth * rows, 2 * lanes), f32),
                pltpu.VMEM((3 * rows, 3 * rows), jnp.bfloat16),
                pltpu.VMEM((3 * lanes, 3 * lanes), jnp.bfloat16),
                pltpu.VMEM((depth * rows, lanes), f32),
                pltpu.VMEM((shots, chunk, lanes), f32),
                pltpu.VMEM((chunk, lanes), f32),
                pltpu.VMEM((length, wide, lanes), f32),
                pltpu.VMEM((3, wide, lanes), f32),
                pltpu.SemaphoreType.DMA((6,)),
                pltpu.SemaphoreType.DMA((5, 2)),
                pltpu.SemaphoreType.DMA((5, 2)),
                pltpu.SemaphoreType.DMA((5,)),
                pltpu.SemaphoreType.DMA((5,)),
                pltpu.SemaphoreType.DMA((2,)),
                pltpu.SemaphoreType.DMA((2,)),
                pltpu.SemaphoreType.DMA((3,)),
                pltpu.SemaphoreType.DMA((3,)),
                pltpu.SemaphoreType.REGULAR,
                pltpu.SemaphoreType.REGULAR((3,)),
            ],
            compiler_params=pltpu.CompilerParams(
                collective_id=0, has_side_effects=True, vmem_limit_bytes=54800 * 1024
            ),
            name="window",
        )(
            stiffness, buoyancy, forward_now, forward_prior, adjoint_now, adjoint_after,
            source_cells, wavelet, receiver_cells, residuals,
        ).reshape(slab)

    placed = (
        P("dom", None, None),
        P("dom", None, None),
        P("shot", "dom", None, None),
        P("shot", "dom", None, None),
        P("shot", "dom", None, None),
        P("shot", "dom", None, None),
        P("shot"),
        P("shot", None),
        P("shot", None),
        P("shot", None, None),
    )
    return jax.shard_map(
        shards, mesh=mesh, in_specs=placed, out_specs=P("dom", None, None), check_vma=False
    )
```

```python
import jax
import jax.numpy as jnp
from jax import lax
from jax.experimental import pallas as pl
from jax.experimental.pallas import tpu as pltpu
from jax.sharding import PartitionSpec as P

C_SECOND = (-205.0 / 72.0, 8.0 / 5.0, -1.0 / 5.0, 8.0 / 315.0, -1.0 / 560.0)
C_FIRST = (4.0 / 5.0, -1.0 / 5.0, 4.0 / 105.0, -1.0 / 280.0)
MESH = pl.DeviceIdType.MESH
WIDTH = 4
P_NOW, SQ_NOW, P_NEXT, SQ_NEXT = range(4)


def make_kernel(shots, doms, depth, rows, lanes, receivers):
    plane = rows * lanes
    half = depth // 2
    length = shots // 2
    chunk = half * rows // shots
    wide = half * rows // length
    band = rows // 2

    def band_rows(part):
        return pl.ds(pl.multiple_of(part * band, band), band)

    steps = sorted({1, length - 1})
    leaps = sorted({2 % length, (length - 2) % length} - {0})

    def kernel(
        stiff_hbm,
        buoy_hbm,
        now_hbm,
        prior_hbm,
        adj_hbm,
        after_hbm,
        source_ref,
        wavelet_ref,
        cells_ref,
        traces_ref,
        out_ref,
        buoy,
        fields,
        stiff,
        prior,
        adj,
        after,
        far_halo,
        near_halo,
        slopes,
        base,
        slope_z,
        image,
        adj_next,
        injected,
        left,
        right,
        grad,
        parts,
        sums,
        load_sem,
        far_send,
        far_recv,
        near_send,
        near_recv,
        share_send,
        share_recv,
        wide_parts,
        wide_sums,
        wide_send,
        wide_recv,
        near_ready,
        pass_send,
        pass_recv,
        greeted,
    ):
        shot = lax.axis_index("shot")
        dom = lax.axis_index("dom")
        core = lax.rem(dom, 2)
        near = dom + 1 - 2 * core
        far = dom - 1 + 2 * core
        has_far = (far >= 0) & (far < doms)
        far_count = jnp.where(has_far, 1, 0)
        outer = core * half
        inner = half - outer
        side = (2 * core - 1).astype(jnp.float32)

        row, column = shot // length, lax.rem(shot, length)

        def along(i):
            return {"shot": row * length + lax.rem(column + i, length)}

        across = {"shot": (1 - row) * length + column}
        line = sorted(range(1, length), key=lambda i: -min(i, length - i))

        barrier = pltpu.get_barrier_semaphore()

        @pl.when(has_far)
        def _():
            pl.semaphore_signal(barrier, 1, device_id={"dom": far}, device_id_type=MESH)

        @pl.when(core == 1)
        def _():
            pl.semaphore_signal(barrier, 1, device_id={"dom": near}, device_id_type=MESH)

        for i in steps:
            pl.semaphore_signal(barrier, 1, device_id=along(i), device_id_type=MESH)
        pl.semaphore_signal(barrier, 1, device_id=across, device_id_type=MESH)

        loads = [
            pltpu.make_async_copy(src, dst, load_sem.at[i])
            for i, (src, dst) in enumerate(
                (
                    (buoy_hbm, buoy.at[pl.ds(WIDTH, depth)]),
                    (now_hbm.at[0], fields.at[P_NOW, pl.ds(WIDTH, depth)]),
                    (stiff_hbm, stiff),
                    (adj_hbm.at[0], adj),
                    (prior_hbm.at[0], prior),
                    (after_hbm.at[0], after),
                )
            )
        ]
        for load in loads:
            load.start()

        blank = jnp.zeros((rows, lanes), jnp.float32)

        def clear(f, carry):
            for z in range(WIDTH):
                fields[f, z] = blank
                fields[f, WIDTH + depth + z] = blank
            return carry

        lax.fori_loop(0, 4, clear, 0)

        def split(value):
            high = value.astype(jnp.bfloat16)
            return high, (value - high.astype(jnp.float32)).astype(jnp.bfloat16)

        def second(offset):
            total = jnp.zeros(offset.shape, jnp.float32)
            for k in range(1, 5):
                total = jnp.where(jnp.abs(offset) == k, C_SECOND[k], total)
            return total

        def first(offset):
            total = jnp.zeros(offset.shape, jnp.float32)
            for k in range(1, 5):
                total = jnp.where(offset == k, C_FIRST[k - 1], total)
                total = jnp.where(offset == -k, -C_FIRST[k - 1], total)
            return total

        def first_extended(source, target, length):
            total = jnp.zeros(source.shape, jnp.float32)
            for k in range(1, 5):
                up = jnp.minimum(target + k, length - 1)
                down = jnp.maximum(target - k, 0)
                total = total + jnp.where(source == up, C_FIRST[k - 1], 0.0)
                total = total - jnp.where(source == down, C_FIRST[k - 1], 0.0)
            return total

        def make_matrices():
            source = lax.broadcasted_iota(jnp.int32, (lanes, lanes), 0)
            target = lax.broadcasted_iota(jnp.int32, (lanes, lanes), 1)
            offset = source - target
            centre = jnp.where(offset == 0, 3.0 * C_SECOND[0], 0.0)
            for at, value in enumerate(
                (second(offset) + centre, first(offset), first_extended(source, target, lanes))
            ):
                columns = pl.ds(at * lanes, lanes)
                high, low = split(value)
                right[0:lanes, columns] = high
                right[lanes : 2 * lanes, columns] = high
                right[2 * lanes : 3 * lanes, columns] = low
            target = lax.broadcasted_iota(jnp.int32, (rows, 3 * rows), 0)
            source = lax.rem(lax.broadcasted_iota(jnp.int32, (rows, 3 * rows), 1), rows)
            last = lax.broadcasted_iota(jnp.int32, (rows, 3 * rows), 1) >= 2 * rows
            offset = source - target
            for at, value in enumerate(
                (second(offset), first(offset), first_extended(source, target, rows))
            ):
                high, low = split(value)
                left[at * rows : (at + 1) * rows] = jnp.where(
                    last, low.astype(jnp.float32), high.astype(jnp.float32)
                ).astype(jnp.bfloat16)

        def dot(a, b):
            return lax.dot_general(
                a, b, (((1,), (0,)), ((), ())), preferred_element_type=jnp.float32
            )

        def differences(value, which):
            high, low = split(value)
            flat_high = high.reshape(2 * rows, lanes)
            flat = jnp.concatenate([flat_high, low.reshape(2 * rows, lanes)], axis=1)
            first_column, columns = (0, 2 * lanes) if which == 0 else (2 * lanes, lanes)
            use = pl.ds(first_column, columns)
            along_y = dot(flat, right[0 : 2 * lanes, use]) + dot(
                flat_high, right[2 * lanes : 3 * lanes, use]
            )
            stacked = jnp.concatenate(
                [jnp.concatenate([high[i], low[i], high[i]], axis=0) for i in range(2)], axis=1
            )
            use = pl.ds(0, 2 * rows) if which == 0 else pl.ds(2 * rows, rows)
            along_x = dot(left[use], stacked)
            return along_x, along_y

        def inject():
            local_cells = cells_ref[...] - dom * (depth * plane)
            cell_rows = jnp.right_shift(local_cells, 7)
            cell_lanes = jnp.bitwise_and(local_cells, lanes - 1)
            lane_hot = lax.broadcasted_iota(jnp.int32, (lanes, receivers), 0) == cell_lanes
            amounts = jnp.concatenate(
                [jnp.where(lane_hot, traces_ref[0, k : k + 1, :], 0.0) for k in range(2)], axis=0
            )
            amounts = amounts.T
            high, _ = split(amounts)
            middle, low = split(amounts - high.astype(jnp.float32))
            row = lax.broadcasted_iota(jnp.int32, (depth * rows, receivers), 0)
            row_hot = jnp.where(row == cell_rows, 1.0, 0.0).astype(jnp.bfloat16)
            injected[...] = dot(row_hot, low) + dot(row_hot, middle) + dot(row_hot, high)

        def scale(z, carry):
            fields[SQ_NOW, WIDTH + z] = stiff[z] * adj[z]
            return carry

        bands = [lax.rem(column + i, 2) for i in range(2)]

        def far_ends(f, part, sending):
            of = band_rows(part)
            if f < 4:
                return far_halo.at[f, pl.ds(0, half), of]
            at = 1 - core if sending else core
            return buoy.at[pl.ds(at * (WIDTH + depth), half), of]

        def far_copy(f, part):
            src = (buoy if f == 4 else fields.at[f]).at[pl.ds(WIDTH + outer, half), band_rows(part)]
            return pltpu.make_async_remote_copy(
                src, far_ends(f, part, True), far_send.at[f, part], far_recv.at[f, part],
                device_id={"dom": far}, device_id_type=MESH,
            )

        def far_arrival(f, part):
            dst = far_ends(f, part, False)
            return pltpu.make_async_remote_copy(
                dst, dst, far_send.at[f, part], far_recv.at[f, part],
                device_id={"dom": far}, device_id_type=MESH,
            )

        def pass_on(part):
            ends = far_ends(4, part, False)
            return pltpu.make_async_remote_copy(
                ends, ends, pass_send, pass_recv,
                device_id={"shot": row * length + column + 1 - 2 * lax.rem(column, 2)}, device_id_type=MESH,
            )

        def near_copy(f):
            if f == 4:
                src = buoy.at[pl.ds(WIDTH + inner, half)]
                dst = buoy.at[pl.ds(core * (WIDTH + depth), half)]
            else:
                src = fields.at[f, pl.ds(WIDTH + inner, half)]
                dst = near_halo.at[f]
            return pltpu.make_async_remote_copy(
                src, dst, near_send.at[f], near_recv.at[f], device_id={"dom": near}, device_id_type=MESH
            )

        def near_arrival(f):
            if f == 4:
                dst = buoy.at[pl.ds((1 - core) * (WIDTH + depth), half)]
            else:
                dst = near_halo.at[f]
            return pltpu.make_async_remote_copy(
                dst, dst, near_send.at[f], near_recv.at[f], device_id={"dom": near}, device_id_type=MESH
            )

        def when_far(act):
            pl.when(has_far)(act)

        def buoy_slopes():
            for z in range(0, depth, 2):
                along_x, along_y = differences(buoy[WIDTH + z : WIDTH + z + 2], 1)
                for i in range(2):
                    slopes[0, z + i] = along_x[:, i * lanes : (i + 1) * lanes]
                    slopes[1, z + i] = along_y[i * rows : (i + 1) * rows]

        def buoy_slope_z(start, use):
            def body(j, carry):
                z = start + j
                along_z = jnp.zeros((use.size, lanes), jnp.float32)
                for k in range(1, 5):
                    up = buoy[WIDTH + z + k, use]
                    down = buoy[WIDTH + z - k, use]
                    along_z = along_z + C_FIRST[k - 1] * (up - down)
                slopes[2, z, use] = along_z
                return carry

            lax.fori_loop(0, half, body, 0)

        def local(f):
            for z0 in range(0, depth, 2):
                along_x, along_y = differences(fields[f, WIDTH + z0 : WIDTH + z0 + 2], 0)
                for i in range(2):
                    z = z0 + i
                    of_x = slice(i * lanes, (i + 1) * lanes)
                    of_y = slice(i * rows, (i + 1) * rows)
                    curve = along_x[0:rows, of_x] + along_y[of_y, 0:lanes]
                    along = jnp.zeros((rows, lanes), jnp.float32)
                    for k in range(1, 5):
                        up = fields[f, WIDTH + z + k]
                        down = fields[f, WIDTH + z - k]
                        curve = curve + C_SECOND[k] * (up + down)
                        along = along + C_FIRST[k - 1] * (up - down)
                    slope_z[f, z] = along
                    base[f, z] = (
                        buoy[WIDTH + z] * curve
                        + along_x[rows : 2 * rows, of_x] * slopes[0, z]
                        + along_y[of_y, lanes : 2 * lanes] * slopes[1, z]
                    )

        make_matrices()
        inject()
        loads[0].wait()
        loads[1].wait()
        pl.semaphore_wait(barrier, len(steps) + 1 + far_count + (1 - core))

        when_far(far_copy(4, bands[0]).start)
        for part in bands:
            when_far(far_copy(P_NOW, part).start)
        loads[2].wait()
        loads[3].wait()
        lax.fori_loop(0, depth, scale, 0)
        for part in bands:
            when_far(far_copy(SQ_NOW, part).start)

        def near_begin():
            @pl.when(core == 0)
            def _():
                pl.semaphore_signal(near_ready, 1, device_id={"dom": near}, device_id_type=MESH)

            @pl.when(core == 1)
            def _():
                pl.semaphore_wait(near_ready, 1)

            for f in (4, P_NOW, SQ_NOW):
                near_copy(f).start()

        pl.when(dom != 1)(near_begin)
        for i in steps:
            pl.semaphore_signal(greeted.at[0], 1, device_id=along(i), device_id_type=MESH)

        buoy_slopes()
        local(P_NOW)
        local(SQ_NOW)

        @pl.when(jnp.logical_not(has_far))
        def _():
            edge = buoy[WIDTH + core * (depth - 1)]
            for z in range(half):
                buoy[core * (WIDTH + depth) + z] = edge
                for f in range(4):
                    far_halo[f, z] = blank

        def whole(f, j, is_far, use):
            halo = far_halo if is_far else near_halo
            up = core if is_far else 1 - core
            z = up * (depth - 1 - j) + (1 - up) * j
            curve = jnp.zeros((use.size, lanes), jnp.float32)
            along = jnp.zeros((use.size, lanes), jnp.float32)
            for k in range(j + 1, 5):
                m = k - j
                plane_at = up * (m - 1) + (1 - up) * (half - m)
                value = halo[f, plane_at, use]
                curve = curve + C_SECOND[k] * value
                along = along + C_FIRST[k - 1] * value
            sign = side if is_far else -side
            along = slope_z[f, z, use] + sign * along
            value = base[f, z, use] + buoy[WIDTH + z, use] * curve + along * slopes[2, z, use]
            return z, value

        for load in loads[4:]:
            load.wait()
        local_source = source_ref[...].reshape(1, 1) - dom * (depth * plane)
        amplitude = wavelet_ref[...]
        everything = pl.ds(0, rows)

        def flat_rows(z, use):
            return pl.ds(pl.multiple_of(z * rows + use.start, band), use.size)

        def forward(is_far, use=everything):
            cell = lax.broadcasted_iota(jnp.int32, (use.size, lanes), 0) * lanes
            cell = cell + lax.broadcasted_iota(jnp.int32, (use.size, lanes), 1)
            for j in range(half):
                z, value = whole(P_NOW, j, is_far, use)
                image[z, use] = value
                here = cell + (z * plane + use.start * lanes)
                shown = jnp.where(here == local_source, amplitude, 0.0)
                fields[P_NEXT, WIDTH + z, use] = (
                    2.0 * fields[P_NOW, WIDTH + z, use] - prior[z, use] + stiff[z, use] * value + shown
                )

        def backward(is_far, use=everything):
            for j in range(half):
                z, value = whole(SQ_NOW, j, is_far, use)
                injected_rows = flat_rows(z, use)
                value = 2.0 * adj[z, use] - after[z, use] + value + injected[injected_rows, 0:lanes]
                adj_next[z, use] = value
                fields[SQ_NEXT, WIDTH + z, use] = stiff[z, use] * value

        def finish(is_far, use=everything):
            for j in range(half):
                z, last_image = whole(P_NEXT, j, is_far, use)
                _, value = whole(SQ_NEXT, j, is_far, use)
                newer = adj_next[z, use]
                flat = flat_rows(z, use)
                value = 2.0 * newer - adj[z, use] + value + injected[flat, lanes : 2 * lanes]
                grad[flat] = newer * last_image + value * image[z, use]

        def share(h, of_row, of_column):
            if h == 0:
                return pl.ds(inner * rows + (of_row * length + of_column) * chunk, chunk)
            at = of_column * chunk
            return pl.ds((outer + at // band) * rows + of_row * band + lax.rem(at, band), chunk)

        def share_copy(h, stage, to_row, i):
            to_column = lax.rem(column + i, length)
            if stage == 0:
                src, dst = grad.at[share(h, to_row, to_column)], parts.at[h, shot]
            else:
                src, dst = sums.at[h], out_ref.at[share(h, row, column)]
            return pltpu.make_async_remote_copy(
                src, dst, share_send.at[h, stage], share_recv.at[h, stage],
                device_id={"shot": to_row * length + to_column}, device_id_type=MESH,
            )

        def share_start(h, stage, to_row):
            for i in line:
                share_copy(h, stage, to_row, i).start()
            pl.when(row != to_row)(share_copy(h, stage, to_row, 0).start)

        def all_shares(h, stage):
            every = parts.at[h, pl.ds(0, shots - 1)]
            return pltpu.make_async_remote_copy(
                every, every, share_send.at[h, stage], share_recv.at[h, stage], device_id=across, device_id_type=MESH
            )

        def add_shares(h):
            all_shares(h, 0).wait_recv()
            total = grad[share(h, row, column)]
            for i in range(1, shots):
                total = total + parts[h, lax.rem(shot + i, shots)]
            sums[h] = total
            for to_row in range(2):
                share_start(h, 1, to_row)
            out_ref[share(h, row, column)] = total

        def wide_share(of):
            return pl.ds(inner * rows + of * wide, wide)

        def wide_copy(stage, i):
            peer = lax.rem(column + i, length)
            if stage == 0:
                src, dst = grad.at[wide_share(peer)], wide_parts.at[column]
            else:
                src, dst = wide_sums.at[2], out_ref.at[wide_share(column)]
            return pltpu.make_async_remote_copy(
                src, dst, wide_send.at[stage], wide_recv.at[stage], device_id=along(i), device_id_type=MESH
            )

        def all_wide(stage):
            every = wide_parts.at[pl.ds(0, length - 1)]
            return pltpu.make_async_remote_copy(
                every, every, wide_send.at[stage], wide_recv.at[stage], device_id=across, device_id_type=MESH
            )

        swap = pltpu.make_async_remote_copy(
            wide_sums.at[0], wide_sums.at[1], wide_send.at[2], wide_recv.at[2], device_id=across, device_id_type=MESH
        )

        def add_wide():
            all_wide(0).wait_recv()
            total = grad[wide_share(column)]
            for i in line:
                total = total + wide_parts[lax.rem(column + i, length)]
            wide_sums[0] = total
            swap.start()
            swap.wait_recv()
            wide_sums[2] = wide_sums[0] + wide_sums[1]
            for i in line:
                wide_copy(1, i).start()
            out_ref[wide_share(column)] = wide_sums[2]

        direct = dom < 2

        def near_fold():
            near_arrival(4).wait_recv()
            buoy_slope_z(inner, everything)
            near_arrival(P_NOW).wait_recv()
            forward(False)
            near_copy(P_NEXT).start()
            near_arrival(SQ_NOW).wait_recv()
            backward(False)
            near_copy(SQ_NEXT).start()

        when_far(far_arrival(4, bands[0]).wait_recv)
        when_far(pass_on(bands[0]).start)
        for part in bands:
            use = band_rows(part)
            if part is bands[1]:
                when_far(pass_on(part).wait_recv)
            buoy_slope_z(outer, use)
            when_far(far_arrival(P_NOW, part).wait_recv)
            forward(True, use)
            when_far(far_copy(P_NEXT, part).start)

        pl.semaphore_wait(greeted.at[0], len(steps))
        for i in leaps:
            pl.semaphore_signal(greeted.at[1], 1, device_id=along(i), device_id_type=MESH)
        pl.when(dom != 1)(near_fold)

        for part in bands:
            when_far(far_arrival(SQ_NOW, part).wait_recv)
            backward(True, band_rows(part))
            when_far(far_copy(SQ_NEXT, part).start)

        @pl.when(dom == 1)
        def _():
            near_begin()
            near_fold()

        if leaps:
            pl.semaphore_wait(greeted.at[1], len(leaps))
        pl.semaphore_signal(greeted.at[2], 1, device_id=across, device_id_type=MESH)

        local(P_NEXT)
        local(SQ_NEXT)
        near_arrival(P_NEXT).wait_recv()
        near_arrival(SQ_NEXT).wait_recv()
        finish(False)
        pl.semaphore_wait(greeted.at[2], 1)

        @pl.when(direct)
        def _():
            for to_row in range(2):
                share_start(0, 0, to_row)

        @pl.when(jnp.logical_not(direct))
        def _():
            for i in line:
                wide_copy(0, i).start()


        for part in bands:
            when_far(far_arrival(P_NEXT, part).wait_recv)
            when_far(far_arrival(SQ_NEXT, part).wait_recv)
            finish(True, band_rows(part))
            share_start(1, 0, part)

        @pl.when(direct)
        def _():
            add_shares(0)

        pl.when(jnp.logical_not(direct))(add_wide)
        add_shares(1)

        for f in range(5):
            for part in bands[: 1 if f == 4 else 2]:
                when_far(far_copy(f, part).wait_send)
            near_copy(f).wait_send()
        when_far(pass_on(bands[0]).wait_send)
        def drain(h):
            for stage in range(2):
                all_shares(h, stage).wait_send()
            all_shares(h, 1).wait_recv()

        @pl.when(direct)
        def _():
            drain(0)

        @pl.when(jnp.logical_not(direct))
        def _():
            for stage in range(2):
                all_wide(stage).wait_send()
            swap.wait_send()
            all_wide(1).wait_recv()

        drain(1)

    return kernel


def solution(mesh):
    shots, doms = mesh.shape["shot"], mesh.shape["dom"]

    def shards(
        stiffness,
        buoyancy,
        forward_now,
        forward_prior,
        adjoint_now,
        adjoint_after,
        source_cells,
        wavelet,
        receiver_cells,
        residuals,
    ):
        depth, rows, lanes = stiffness.shape
        receivers = receiver_cells.shape[1]
        half = depth // 2
        chunk = half * rows // shots
        wide = 2 * chunk
        padded = (depth + 2 * WIDTH, rows, lanes)
        slab = (depth, rows, lanes)
        f32 = jnp.float32
        in_hbm = pl.BlockSpec(memory_space=pltpu.HBM)
        return pl.pallas_call(
            make_kernel(shots, doms, depth, rows, lanes, receivers),
            out_shape=jax.ShapeDtypeStruct((depth * rows, lanes), f32),
            in_specs=[in_hbm] * 6 + [pl.BlockSpec(memory_space=pltpu.VMEM)] * 4,
            out_specs=pl.BlockSpec(memory_space=pltpu.VMEM),
            scratch_shapes=[
                pltpu.VMEM(padded, f32),
                pltpu.VMEM((4, *padded), f32),
                pltpu.VMEM(slab, f32),
                pltpu.VMEM(slab, f32),
                pltpu.VMEM(slab, f32),
                pltpu.VMEM(slab, f32),
                pltpu.VMEM((4, half, rows, lanes), f32),
                pltpu.VMEM((4, half, rows, lanes), f32),
                pltpu.VMEM((3, *slab), f32),
                pltpu.VMEM((4, *slab), f32),
                pltpu.VMEM((4, *slab), f32),
                pltpu.VMEM(slab, f32),
                pltpu.VMEM(slab, f32),
                pltpu.VMEM((depth * rows, 2 * lanes), f32),
                pltpu.VMEM((3 * rows, 3 * rows), jnp.bfloat16),
                pltpu.VMEM((3 * lanes, 3 * lanes), jnp.bfloat16),
                pltpu.VMEM((depth * rows, lanes), f32),
                pltpu.VMEM((2, shots, chunk, lanes), f32),
                pltpu.VMEM((2, chunk, lanes), f32),
                pltpu.SemaphoreType.DMA((6,)),
                pltpu.SemaphoreType.DMA((5, 2)),
                pltpu.SemaphoreType.DMA((5, 2)),
                pltpu.SemaphoreType.DMA((5,)),
                pltpu.SemaphoreType.DMA((5,)),
                pltpu.SemaphoreType.DMA((2, 2)),
                pltpu.SemaphoreType.DMA((2, 2)),
                pltpu.VMEM((shots // 2, wide, lanes), f32),
                pltpu.VMEM((3, wide, lanes), f32),
                pltpu.SemaphoreType.DMA((3,)),
                pltpu.SemaphoreType.DMA((3,)),
                pltpu.SemaphoreType.REGULAR,
                pltpu.SemaphoreType.DMA,
                pltpu.SemaphoreType.DMA,
                pltpu.SemaphoreType.REGULAR((3,)),
            ],
            compiler_params=pltpu.CompilerParams(
                collective_id=0, has_side_effects=True, vmem_limit_bytes=54800 * 1024
            ),
            name="window",
        )(
            stiffness, buoyancy, forward_now, forward_prior, adjoint_now, adjoint_after,
            source_cells, wavelet, receiver_cells, residuals,
        ).reshape(slab)

    placed = (
        P("dom", None, None),
        P("dom", None, None),
        P("shot", "dom", None, None),
        P("shot", "dom", None, None),
        P("shot", "dom", None, None),
        P("shot", "dom", None, None),
        P("shot"),
        P("shot", None),
        P("shot", None),
        P("shot", None, None),
    )
    return jax.shard_map(
        shards, mesh=mesh, in_specs=placed, out_specs=P("dom", None, None), check_vma=False
    )
```

```python
import jax
import jax.numpy as jnp
from jax import lax
from jax.experimental import pallas as pl
from jax.experimental.pallas import tpu as pltpu
from jax.sharding import PartitionSpec as P

C_SECOND = (-205.0 / 72.0, 8.0 / 5.0, -1.0 / 5.0, 8.0 / 315.0, -1.0 / 560.0)
C_FIRST = (4.0 / 5.0, -1.0 / 5.0, 4.0 / 105.0, -1.0 / 280.0)
MESH = pl.DeviceIdType.MESH
WIDTH = 4
P_NOW, SQ_NOW, P_NEXT, SQ_NEXT = range(4)


def make_kernel(shots, doms, depth, rows, lanes, receivers):
    plane = rows * lanes
    half = depth // 2
    length = shots // 2
    chunk = half * rows // shots
    wide = half * rows // length
    band = rows // 2

    def band_rows(part):
        return pl.ds(pl.multiple_of(part * band, band), band)

    steps = sorted({1, length - 1})
    leaps = sorted({2 % length, (length - 2) % length} - {0})

    def kernel(
        stiff_hbm,
        buoy_hbm,
        now_hbm,
        prior_hbm,
        adj_hbm,
        after_hbm,
        source_any,
        wavelet_any,
        cells_any,
        traces_any,
        out_ref,
        source_ref,
        wavelet_ref,
        cells_ref,
        traces_ref,
        buoy,
        fields,
        stiff,
        prior,
        adj,
        after,
        far_halo,
        near_halo,
        slopes,
        base,
        slope_z,
        image,
        adj_next,
        injected,
        left,
        right,
        grad,
        parts,
        sums,
        load_sem,
        own_sem,
        far_send,
        far_recv,
        near_send,
        near_recv,
        share_send,
        share_recv,
        wide_parts,
        wide_sums,
        wide_send,
        wide_recv,
        near_ready,
        pass_send,
        pass_recv,
        greeted,
    ):
        shot = lax.axis_index("shot")
        dom = lax.axis_index("dom")
        core = lax.rem(dom, 2)
        near = dom + 1 - 2 * core
        far = dom - 1 + 2 * core
        has_far = (far >= 0) & (far < doms)
        far_count = jnp.where(has_far, 1, 0)
        outer = core * half
        inner = half - outer
        side = (2 * core - 1).astype(jnp.float32)

        row, column = shot // length, lax.rem(shot, length)

        def along(i):
            return {"shot": row * length + lax.rem(column + i, length)}

        across = {"shot": (1 - row) * length + column}
        line = sorted(range(1, length), key=lambda i: -min(i, length - i))

        barrier = pltpu.get_barrier_semaphore()

        @pl.when(has_far)
        def _():
            pl.semaphore_signal(barrier, 1, device_id={"dom": far}, device_id_type=MESH)

        @pl.when(core == 1)
        def _():
            pl.semaphore_signal(barrier, 1, device_id={"dom": near}, device_id_type=MESH)

        for i in steps:
            pl.semaphore_signal(barrier, 1, device_id=along(i), device_id_type=MESH)
        pl.semaphore_signal(barrier, 1, device_id=across, device_id_type=MESH)

        loads = [
            pltpu.make_async_copy(src, dst, load_sem.at[i])
            for i, (src, dst) in enumerate(
                (
                    (buoy_hbm, buoy.at[pl.ds(WIDTH, depth)]),
                    (now_hbm.at[0], fields.at[P_NOW, pl.ds(WIDTH, depth)]),
                    (stiff_hbm, stiff),
                    (adj_hbm.at[0], adj),
                    (prior_hbm.at[0], prior),
                    (after_hbm.at[0], after),
                    (cells_any, cells_ref),
                    (traces_any, traces_ref),
                    (source_any, source_ref),
                    (wavelet_any, wavelet_ref),
                )
            )
        ]
        for load in loads:
            load.start()

        blank = jnp.zeros((rows, lanes), jnp.float32)

        def clear(f, carry):
            for z in range(WIDTH):
                fields[f, z] = blank
                fields[f, WIDTH + depth + z] = blank
            return carry

        lax.fori_loop(0, 4, clear, 0)

        def split(value):
            high = value.astype(jnp.bfloat16)
            return high, (value - high.astype(jnp.float32)).astype(jnp.bfloat16)

        def second(offset):
            total = jnp.zeros(offset.shape, jnp.float32)
            for k in range(1, 5):
                total = jnp.where(jnp.abs(offset) == k, C_SECOND[k], total)
            return total

        def first(offset):
            total = jnp.zeros(offset.shape, jnp.float32)
            for k in range(1, 5):
                total = jnp.where(offset == k, C_FIRST[k - 1], total)
                total = jnp.where(offset == -k, -C_FIRST[k - 1], total)
            return total

        def first_extended(source, target, length):
            total = jnp.zeros(source.shape, jnp.float32)
            for k in range(1, 5):
                up = jnp.minimum(target + k, length - 1)
                down = jnp.maximum(target - k, 0)
                total = total + jnp.where(source == up, C_FIRST[k - 1], 0.0)
                total = total - jnp.where(source == down, C_FIRST[k - 1], 0.0)
            return total

        def make_matrices():
            source = lax.broadcasted_iota(jnp.int32, (lanes, lanes), 0)
            target = lax.broadcasted_iota(jnp.int32, (lanes, lanes), 1)
            offset = source - target
            centre = jnp.where(offset == 0, 3.0 * C_SECOND[0], 0.0)
            for at, value in enumerate(
                (second(offset) + centre, first(offset), first_extended(source, target, lanes))
            ):
                columns = pl.ds(at * lanes, lanes)
                high, low = split(value)
                right[0:lanes, columns] = high
                right[lanes : 2 * lanes, columns] = high
                right[2 * lanes : 3 * lanes, columns] = low
            target = lax.broadcasted_iota(jnp.int32, (rows, 3 * rows), 0)
            source = lax.rem(lax.broadcasted_iota(jnp.int32, (rows, 3 * rows), 1), rows)
            last = lax.broadcasted_iota(jnp.int32, (rows, 3 * rows), 1) >= 2 * rows
            offset = source - target
            for at, value in enumerate(
                (second(offset), first(offset), first_extended(source, target, rows))
            ):
                high, low = split(value)
                left[at * rows : (at + 1) * rows] = jnp.where(
                    last, low.astype(jnp.float32), high.astype(jnp.float32)
                ).astype(jnp.bfloat16)

        def dot(a, b):
            return lax.dot_general(
                a, b, (((1,), (0,)), ((), ())), preferred_element_type=jnp.float32
            )

        def differences(value, which):
            high, low = split(value)
            flat_high = high.reshape(2 * rows, lanes)
            flat = jnp.concatenate([flat_high, low.reshape(2 * rows, lanes)], axis=1)
            first_column, columns = (0, 2 * lanes) if which == 0 else (2 * lanes, lanes)
            use = pl.ds(first_column, columns)
            along_y = dot(flat, right[0 : 2 * lanes, use]) + dot(
                flat_high, right[2 * lanes : 3 * lanes, use]
            )
            stacked = jnp.concatenate(
                [jnp.concatenate([high[i], low[i], high[i]], axis=0) for i in range(2)], axis=1
            )
            use = pl.ds(0, 2 * rows) if which == 0 else pl.ds(2 * rows, rows)
            along_x = dot(left[use], stacked)
            return along_x, along_y

        def inject():
            local_cells = cells_ref[...] - dom * (depth * plane)
            cell_rows = jnp.right_shift(local_cells, 7)
            cell_lanes = jnp.bitwise_and(local_cells, lanes - 1)
            lane_hot = lax.broadcasted_iota(jnp.int32, (lanes, receivers), 0) == cell_lanes
            amounts = jnp.concatenate(
                [jnp.where(lane_hot, traces_ref[0, k : k + 1, :], 0.0) for k in range(2)], axis=0
            )
            amounts = amounts.T
            high, _ = split(amounts)
            middle, low = split(amounts - high.astype(jnp.float32))
            row = lax.broadcasted_iota(jnp.int32, (depth * rows, receivers), 0)
            row_hot = jnp.where(row == cell_rows, 1.0, 0.0).astype(jnp.bfloat16)
            injected[...] = dot(row_hot, low) + dot(row_hot, middle) + dot(row_hot, high)

        def scale(z, carry):
            fields[SQ_NOW, WIDTH + z] = stiff[z] * adj[z]
            return carry

        bands = [lax.rem(column + i, 2) for i in range(2)]

        def far_ends(f, part, sending):
            of = band_rows(part)
            if f < 4:
                return far_halo.at[f, pl.ds(0, half), of]
            at = 1 - core if sending else core
            return buoy.at[pl.ds(at * (WIDTH + depth), half), of]

        def far_copy(f, part):
            src = (buoy if f == 4 else fields.at[f]).at[pl.ds(WIDTH + outer, half), band_rows(part)]
            return pltpu.make_async_remote_copy(
                src, far_ends(f, part, True), far_send.at[f, part], far_recv.at[f, part],
                device_id={"dom": far}, device_id_type=MESH,
            )

        def far_arrival(f, part):
            dst = far_ends(f, part, False)
            return pltpu.make_async_remote_copy(
                dst, dst, far_send.at[f, part], far_recv.at[f, part],
                device_id={"dom": far}, device_id_type=MESH,
            )

        def pass_on(part):
            ends = far_ends(4, part, False)
            return pltpu.make_async_remote_copy(
                ends, ends, pass_send, pass_recv,
                device_id={"shot": row * length + column + 1 - 2 * lax.rem(column, 2)}, device_id_type=MESH,
            )

        def near_copy(f):
            if f == 4:
                src = buoy.at[pl.ds(WIDTH + inner, half)]
                dst = buoy.at[pl.ds(core * (WIDTH + depth), half)]
            else:
                src = fields.at[f, pl.ds(WIDTH + inner, half)]
                dst = near_halo.at[f]
            return pltpu.make_async_remote_copy(
                src, dst, near_send.at[f], near_recv.at[f], device_id={"dom": near}, device_id_type=MESH
            )

        def near_arrival(f):
            if f == 4:
                dst = buoy.at[pl.ds((1 - core) * (WIDTH + depth), half)]
            else:
                dst = near_halo.at[f]
            return pltpu.make_async_remote_copy(
                dst, dst, near_send.at[f], near_recv.at[f], device_id={"dom": near}, device_id_type=MESH
            )

        def when_far(act):
            pl.when(has_far)(act)

        def buoy_slopes():
            for z in range(0, depth, 2):
                along_x, along_y = differences(buoy[WIDTH + z : WIDTH + z + 2], 1)
                for i in range(2):
                    slopes[0, z + i] = along_x[:, i * lanes : (i + 1) * lanes]
                    slopes[1, z + i] = along_y[i * rows : (i + 1) * rows]

        def buoy_slope_z(start, use):
            def body(j, carry):
                z = start + j
                along_z = jnp.zeros((use.size, lanes), jnp.float32)
                for k in range(1, 5):
                    up = buoy[WIDTH + z + k, use]
                    down = buoy[WIDTH + z - k, use]
                    along_z = along_z + C_FIRST[k - 1] * (up - down)
                slopes[2, z, use] = along_z
                return carry

            lax.fori_loop(0, half, body, 0)

        def local(f):
            for z0 in range(0, depth, 2):
                along_x, along_y = differences(fields[f, WIDTH + z0 : WIDTH + z0 + 2], 0)
                for i in range(2):
                    z = z0 + i
                    of_x = slice(i * lanes, (i + 1) * lanes)
                    of_y = slice(i * rows, (i + 1) * rows)
                    curve = along_x[0:rows, of_x] + along_y[of_y, 0:lanes]
                    along = jnp.zeros((rows, lanes), jnp.float32)
                    for k in range(1, 5):
                        up = fields[f, WIDTH + z + k]
                        down = fields[f, WIDTH + z - k]
                        curve = curve + C_SECOND[k] * (up + down)
                        along = along + C_FIRST[k - 1] * (up - down)
                    slope_z[f, z] = along
                    base[f, z] = (
                        buoy[WIDTH + z] * curve
                        + along_x[rows : 2 * rows, of_x] * slopes[0, z]
                        + along_y[of_y, lanes : 2 * lanes] * slopes[1, z]
                    )

        make_matrices()
        loads[0].wait()
        loads[1].wait()
        pl.semaphore_wait(barrier, len(steps) + 1 + far_count + (1 - core))

        when_far(far_copy(4, bands[0]).start)
        for part in bands:
            when_far(far_copy(P_NOW, part).start)
        loads[2].wait()
        loads[3].wait()
        lax.fori_loop(0, depth, scale, 0)
        for part in bands:
            when_far(far_copy(SQ_NOW, part).start)

        def near_begin():
            @pl.when(core == 0)
            def _():
                pl.semaphore_signal(near_ready, 1, device_id={"dom": near}, device_id_type=MESH)

            @pl.when(core == 1)
            def _():
                pl.semaphore_wait(near_ready, 1)

            for f in (4, P_NOW, SQ_NOW):
                near_copy(f).start()

        pl.when(dom != 1)(near_begin)
        for i in steps:
            pl.semaphore_signal(greeted.at[0], 1, device_id=along(i), device_id_type=MESH)

        buoy_slopes()
        local(P_NOW)
        local(SQ_NOW)
        loads[6].wait()
        loads[7].wait()
        inject()

        @pl.when(jnp.logical_not(has_far))
        def _():
            edge = buoy[WIDTH + core * (depth - 1)]
            for z in range(half):
                buoy[core * (WIDTH + depth) + z] = edge
                for f in range(4):
                    far_halo[f, z] = blank

        def whole(f, j, is_far, use):
            halo = far_halo if is_far else near_halo
            up = core if is_far else 1 - core
            z = up * (depth - 1 - j) + (1 - up) * j
            curve = jnp.zeros((use.size, lanes), jnp.float32)
            along = jnp.zeros((use.size, lanes), jnp.float32)
            for k in range(j + 1, 5):
                m = k - j
                plane_at = up * (m - 1) + (1 - up) * (half - m)
                value = halo[f, plane_at, use]
                curve = curve + C_SECOND[k] * value
                along = along + C_FIRST[k - 1] * value
            sign = side if is_far else -side
            along = slope_z[f, z, use] + sign * along
            value = base[f, z, use] + buoy[WIDTH + z, use] * curve + along * slopes[2, z, use]
            return z, value

        for i in (4, 5, 8, 9):
            loads[i].wait()
        local_source = source_ref[0] - dom * (depth * plane)
        amplitude = wavelet_ref[0, 0]
        everything = pl.ds(0, rows)

        def flat_rows(z, use):
            return pl.ds(pl.multiple_of(z * rows + use.start, band), use.size)

        def forward(is_far, use=everything):
            cell = lax.broadcasted_iota(jnp.int32, (use.size, lanes), 0) * lanes
            cell = cell + lax.broadcasted_iota(jnp.int32, (use.size, lanes), 1)
            for j in range(half):
                z, value = whole(P_NOW, j, is_far, use)
                image[z, use] = value
                here = cell + (z * plane + use.start * lanes)
                shown = jnp.where(here == local_source, amplitude, 0.0)
                fields[P_NEXT, WIDTH + z, use] = (
                    2.0 * fields[P_NOW, WIDTH + z, use] - prior[z, use] + stiff[z, use] * value + shown
                )

        def backward(is_far, use=everything):
            for j in range(half):
                z, value = whole(SQ_NOW, j, is_far, use)
                injected_rows = flat_rows(z, use)
                value = 2.0 * adj[z, use] - after[z, use] + value + injected[injected_rows, 0:lanes]
                adj_next[z, use] = value
                fields[SQ_NEXT, WIDTH + z, use] = stiff[z, use] * value

        def finish(is_far, use=everything):
            for j in range(half):
                z, last_image = whole(P_NEXT, j, is_far, use)
                _, value = whole(SQ_NEXT, j, is_far, use)
                newer = adj_next[z, use]
                flat = flat_rows(z, use)
                value = 2.0 * newer - adj[z, use] + value + injected[flat, lanes : 2 * lanes]
                grad[flat] = newer * last_image + value * image[z, use]

        def share(h, of_row, of_column):
            if h == 0:
                return pl.ds(inner * rows + (of_row * length + of_column) * chunk, chunk)
            at = of_column * chunk
            return pl.ds((outer + at // band) * rows + of_row * band + lax.rem(at, band), chunk)

        def share_copy(h, stage, to_row, i):
            to_column = lax.rem(column + i, length)
            if stage == 0:
                src, dst = grad.at[share(h, to_row, to_column)], parts.at[h, shot]
            else:
                src, dst = sums.at[h], out_ref.at[share(h, row, column)]
            return pltpu.make_async_remote_copy(
                src, dst, share_send.at[h, stage], share_recv.at[h, stage],
                device_id={"shot": to_row * length + to_column}, device_id_type=MESH,
            )

        def share_start(h, stage, to_row):
            for i in line:
                share_copy(h, stage, to_row, i).start()
            pl.when(row != to_row)(share_copy(h, stage, to_row, 0).start)

        def all_shares(h, stage):
            every = parts.at[h, pl.ds(0, shots - 1)]
            return pltpu.make_async_remote_copy(
                every, every, share_send.at[h, stage], share_recv.at[h, stage], device_id=across, device_id_type=MESH
            )

        def add_shares(h):
            all_shares(h, 0).wait_recv()
            total = grad[share(h, row, column)]
            for i in range(1, shots):
                total = total + parts[h, lax.rem(shot + i, shots)]
            sums[h] = total
            share_copy(h, 1, 1 - row, length // 2).start()
            for i in line:
                share_copy(h, 1, row, i).start()
                if i != length // 2:
                    share_copy(h, 1, 1 - row, i).start()
            share_copy(h, 1, 1 - row, 0).start()
            pltpu.make_async_copy(sums.at[h], out_ref.at[share(h, row, column)], own_sem.at[h]).start()

        def wide_share(of):
            return pl.ds(inner * rows + of * wide, wide)

        def wide_copy(stage, i):
            peer = lax.rem(column + i, length)
            if stage == 0:
                src, dst = grad.at[wide_share(peer)], wide_parts.at[column]
            else:
                src, dst = wide_sums.at[2], out_ref.at[wide_share(column)]
            return pltpu.make_async_remote_copy(
                src, dst, wide_send.at[stage], wide_recv.at[stage], device_id=along(i), device_id_type=MESH
            )

        def all_wide(stage):
            every = wide_parts.at[pl.ds(0, length - 1)]
            return pltpu.make_async_remote_copy(
                every, every, wide_send.at[stage], wide_recv.at[stage], device_id=across, device_id_type=MESH
            )

        swap = pltpu.make_async_remote_copy(
            wide_sums.at[0], wide_sums.at[1], wide_send.at[2], wide_recv.at[2], device_id=across, device_id_type=MESH
        )

        def swap_wide():
            all_wide(0).wait_recv()
            total = grad[wide_share(column)]
            for i in line:
                total = total + wide_parts[lax.rem(column + i, length)]
            wide_sums[0] = total
            swap.start()

        def add_wide():
            swap.wait_recv()
            wide_sums[2] = wide_sums[0] + wide_sums[1]
            for i in line:
                wide_copy(1, i).start()
            pltpu.make_async_copy(wide_sums.at[2], out_ref.at[wide_share(column)], own_sem.at[2]).start()

        direct = dom < 2

        def near_fold():
            near_arrival(4).wait_recv()
            buoy_slope_z(inner, everything)
            near_arrival(P_NOW).wait_recv()
            forward(False)
            near_copy(P_NEXT).start()
            near_arrival(SQ_NOW).wait_recv()
            backward(False)
            near_copy(SQ_NEXT).start()

        pl.when(dom != 1)(near_fold)
        pl.semaphore_wait(greeted.at[0], len(steps))
        for i in leaps:
            pl.semaphore_signal(greeted.at[1], 1, device_id=along(i), device_id_type=MESH)
        when_far(far_arrival(4, bands[0]).wait_recv)
        when_far(pass_on(bands[0]).start)
        if leaps:
            pl.semaphore_wait(greeted.at[1], len(leaps))
        pl.semaphore_signal(greeted.at[2], 1, device_id=across, device_id_type=MESH)
        for part in bands:
            use = band_rows(part)
            if part is bands[1]:
                when_far(pass_on(part).wait_recv)
            buoy_slope_z(outer, use)
            when_far(far_arrival(P_NOW, part).wait_recv)
            forward(True, use)
            when_far(far_copy(P_NEXT, part).start)

        pl.when(dom != 1)(lambda: local(P_NEXT))

        for part in bands:
            when_far(far_arrival(SQ_NOW, part).wait_recv)
            backward(True, band_rows(part))
            when_far(far_copy(SQ_NEXT, part).start)

        @pl.when(dom == 1)
        def _():
            near_begin()
            near_fold()
            local(P_NEXT)

        local(SQ_NEXT)
        near_arrival(P_NEXT).wait_recv()
        near_arrival(SQ_NEXT).wait_recv()
        finish(False)

        pl.semaphore_wait(greeted.at[2], 1)

        @pl.when(direct)
        def _():
            for to_row in range(2):
                share_start(0, 0, to_row)

        @pl.when(jnp.logical_not(direct))
        def _():
            for i in line:
                wide_copy(0, i).start()


        for part in bands:
            when_far(far_arrival(P_NEXT, part).wait_recv)
            when_far(far_arrival(SQ_NEXT, part).wait_recv)
            finish(True, band_rows(part))
            share_start(1, 0, part)
            if part is bands[0]:
                pl.when(jnp.logical_not(direct))(swap_wide)

        @pl.when(direct)
        def _():
            add_shares(0)

        pl.when(jnp.logical_not(direct))(add_wide)
        add_shares(1)

        for f in range(5):
            for part in bands[: 1 if f == 4 else 2]:
                when_far(far_copy(f, part).wait_send)
            near_copy(f).wait_send()
        when_far(pass_on(bands[0]).wait_send)
        def drain(h):
            for stage in range(2):
                all_shares(h, stage).wait_send()
            pltpu.make_async_copy(sums.at[h], out_ref.at[share(h, row, column)], own_sem.at[h]).wait()
            all_shares(h, 1).wait_recv()

        @pl.when(direct)
        def _():
            drain(0)

        @pl.when(jnp.logical_not(direct))
        def _():
            for stage in range(2):
                all_wide(stage).wait_send()
            swap.wait_send()
            pltpu.make_async_copy(wide_sums.at[2], out_ref.at[wide_share(column)], own_sem.at[2]).wait()
            all_wide(1).wait_recv()

        drain(1)

    return kernel


def solution(mesh):
    shots, doms = mesh.shape["shot"], mesh.shape["dom"]

    def shards(
        stiffness,
        buoyancy,
        forward_now,
        forward_prior,
        adjoint_now,
        adjoint_after,
        source_cells,
        wavelet,
        receiver_cells,
        residuals,
    ):
        depth, rows, lanes = stiffness.shape
        receivers = receiver_cells.shape[1]
        half = depth // 2
        chunk = half * rows // shots
        wide = 2 * chunk
        padded = (depth + 2 * WIDTH, rows, lanes)
        slab = (depth, rows, lanes)
        f32 = jnp.float32
        in_hbm = pl.BlockSpec(memory_space=pltpu.HBM)
        in_any = pl.BlockSpec(memory_space=pl.ANY)
        return pl.pallas_call(
            make_kernel(shots, doms, depth, rows, lanes, receivers),
            out_shape=jax.ShapeDtypeStruct((depth * rows, lanes), f32),
            in_specs=[in_hbm] * 6 + [in_any] * 4,
            out_specs=in_any,
            scratch_shapes=[
                pltpu.SMEM((1,), jnp.int32),
                pltpu.SMEM((1, 1), f32),
                pltpu.VMEM((1, receivers), jnp.int32),
                pltpu.VMEM((1, 2, receivers), f32),
                pltpu.VMEM(padded, f32),
                pltpu.VMEM((4, *padded), f32),
                pltpu.VMEM(slab, f32),
                pltpu.VMEM(slab, f32),
                pltpu.VMEM(slab, f32),
                pltpu.VMEM(slab, f32),
                pltpu.VMEM((4, half, rows, lanes), f32),
                pltpu.VMEM((4, half, rows, lanes), f32),
                pltpu.VMEM((3, *slab), f32),
                pltpu.VMEM((4, *slab), f32),
                pltpu.VMEM((4, *slab), f32),
                pltpu.VMEM(slab, f32),
                pltpu.VMEM(slab, f32),
                pltpu.VMEM((depth * rows, 2 * lanes), f32),
                pltpu.VMEM((3 * rows, 3 * rows), jnp.bfloat16),
                pltpu.VMEM((3 * lanes, 3 * lanes), jnp.bfloat16),
                pltpu.VMEM((depth * rows, lanes), f32),
                pltpu.VMEM((2, shots, chunk, lanes), f32),
                pltpu.VMEM((2, chunk, lanes), f32),
                pltpu.SemaphoreType.DMA((10,)),
                pltpu.SemaphoreType.DMA((3,)),
                pltpu.SemaphoreType.DMA((5, 2)),
                pltpu.SemaphoreType.DMA((5, 2)),
                pltpu.SemaphoreType.DMA((5,)),
                pltpu.SemaphoreType.DMA((5,)),
                pltpu.SemaphoreType.DMA((2, 2)),
                pltpu.SemaphoreType.DMA((2, 2)),
                pltpu.VMEM((shots // 2, wide, lanes), f32),
                pltpu.VMEM((3, wide, lanes), f32),
                pltpu.SemaphoreType.DMA((3,)),
                pltpu.SemaphoreType.DMA((3,)),
                pltpu.SemaphoreType.REGULAR,
                pltpu.SemaphoreType.DMA,
                pltpu.SemaphoreType.DMA,
                pltpu.SemaphoreType.REGULAR((3,)),
            ],
            compiler_params=pltpu.CompilerParams(
                collective_id=0, has_side_effects=True, vmem_limit_bytes=54800 * 1024
            ),
            name="window",
        )(
            stiffness, buoyancy, forward_now, forward_prior, adjoint_now, adjoint_after,
            source_cells, wavelet, receiver_cells, residuals,
        ).reshape(slab)

    placed = (
        P("dom", None, None),
        P("dom", None, None),
        P("shot", "dom", None, None),
        P("shot", "dom", None, None),
        P("shot", "dom", None, None),
        P("shot", "dom", None, None),
        P("shot"),
        P("shot", None),
        P("shot", None),
        P("shot", None, None),
    )
    return jax.shard_map(
        shards, mesh=mesh, in_specs=placed, out_specs=P("dom", None, None), check_vma=False
    )
```

```python
import jax
import jax.numpy as jnp
from jax import lax
from jax.experimental import pallas as pl
from jax.experimental.pallas import tpu as pltpu
from jax.sharding import PartitionSpec as P

C_SECOND = (-205.0 / 72.0, 8.0 / 5.0, -1.0 / 5.0, 8.0 / 315.0, -1.0 / 560.0)
C_FIRST = (4.0 / 5.0, -1.0 / 5.0, 4.0 / 105.0, -1.0 / 280.0)
MESH = pl.DeviceIdType.MESH
WIDTH = 4
P_NOW, SQ_NOW, P_NEXT, SQ_NEXT = range(4)


def make_kernel(shots, doms, depth, rows, lanes, receivers):
    plane = rows * lanes
    half = depth // 2
    length = shots // 2
    chunk = half * rows // shots
    wide = half * rows // length
    band = rows // 2

    def band_rows(part):
        return pl.ds(pl.multiple_of(part * band, band), band)

    steps = sorted({1, length - 1})
    leaps = sorted({2 % length, (length - 2) % length} - {0})

    def kernel(
        stiff_hbm,
        buoy_hbm,
        now_hbm,
        prior_hbm,
        adj_hbm,
        after_hbm,
        source_any,
        wavelet_any,
        cells_any,
        traces_any,
        out_ref,
        source_ref,
        wavelet_ref,
        cells_ref,
        traces_ref,
        buoy,
        fields,
        stiff,
        prior,
        adj,
        after,
        far_halo,
        near_halo,
        slopes,
        base,
        slope_z,
        image,
        adj_next,
        injected,
        left,
        right,
        grad,
        parts,
        sums,
        load_sem,
        own_sem,
        far_send,
        far_recv,
        near_send,
        near_recv,
        share_send,
        share_recv,
        wide_parts,
        wide_sums,
        wide_send,
        wide_recv,
        near_ready,
        pass_send,
        pass_recv,
        greeted,
    ):
        shot = lax.axis_index("shot")
        dom = lax.axis_index("dom")
        core = lax.rem(dom, 2)
        near = dom + 1 - 2 * core
        far = dom - 1 + 2 * core
        has_far = (far >= 0) & (far < doms)
        far_count = jnp.where(has_far, 1, 0)
        outer = core * half
        inner = half - outer
        side = (2 * core - 1).astype(jnp.float32)

        row, column = shot // length, lax.rem(shot, length)

        def along(i):
            return {"shot": row * length + lax.rem(column + i, length)}

        across = {"shot": (1 - row) * length + column}
        line = sorted(range(1, length), key=lambda i: -min(i, length - i))

        barrier = pltpu.get_barrier_semaphore()

        @pl.when(has_far)
        def _():
            pl.semaphore_signal(barrier, 1, device_id={"dom": far}, device_id_type=MESH)

        @pl.when(core == 1)
        def _():
            pl.semaphore_signal(barrier, 1, device_id={"dom": near}, device_id_type=MESH)

        for i in steps:
            pl.semaphore_signal(barrier, 1, device_id=along(i), device_id_type=MESH)
        pl.semaphore_signal(barrier, 1, device_id=across, device_id_type=MESH)

        loads = [
            pltpu.make_async_copy(src, dst, load_sem.at[i])
            for i, (src, dst) in enumerate(
                (
                    (buoy_hbm, buoy.at[pl.ds(WIDTH, depth)]),
                    (now_hbm.at[0], fields.at[P_NOW, pl.ds(WIDTH, depth)]),
                    (stiff_hbm, stiff),
                    (adj_hbm.at[0], adj),
                    (prior_hbm.at[0], prior),
                    (after_hbm.at[0], after),
                    (cells_any, cells_ref),
                    (traces_any, traces_ref),
                    (source_any, source_ref),
                    (wavelet_any, wavelet_ref),
                )
            )
        ]
        for load in loads:
            load.start()

        blank = jnp.zeros((rows, lanes), jnp.float32)

        def clear(f, carry):
            for z in range(WIDTH):
                fields[f, z] = blank
                fields[f, WIDTH + depth + z] = blank
            return carry

        lax.fori_loop(0, 4, clear, 0)

        def split(value):
            high = value.astype(jnp.bfloat16)
            return high, (value - high.astype(jnp.float32)).astype(jnp.bfloat16)

        def second(offset):
            total = jnp.zeros(offset.shape, jnp.float32)
            for k in range(1, 5):
                total = jnp.where(jnp.abs(offset) == k, C_SECOND[k], total)
            return total

        def first(offset):
            total = jnp.zeros(offset.shape, jnp.float32)
            for k in range(1, 5):
                total = jnp.where(offset == k, C_FIRST[k - 1], total)
                total = jnp.where(offset == -k, -C_FIRST[k - 1], total)
            return total

        def first_extended(source, target, length):
            total = jnp.zeros(source.shape, jnp.float32)
            for k in range(1, 5):
                up = jnp.minimum(target + k, length - 1)
                down = jnp.maximum(target - k, 0)
                total = total + jnp.where(source == up, C_FIRST[k - 1], 0.0)
                total = total - jnp.where(source == down, C_FIRST[k - 1], 0.0)
            return total

        def make_matrices():
            source = lax.broadcasted_iota(jnp.int32, (lanes, lanes), 0)
            target = lax.broadcasted_iota(jnp.int32, (lanes, lanes), 1)
            offset = source - target
            centre = jnp.where(offset == 0, 3.0 * C_SECOND[0], 0.0)
            for at, value in enumerate(
                (second(offset) + centre, first(offset), first_extended(source, target, lanes))
            ):
                columns = pl.ds(at * lanes, lanes)
                high, low = split(value)
                right[0:lanes, columns] = high
                right[lanes : 2 * lanes, columns] = high
                right[2 * lanes : 3 * lanes, columns] = low
            target = lax.broadcasted_iota(jnp.int32, (rows, 3 * rows), 0)
            source = lax.rem(lax.broadcasted_iota(jnp.int32, (rows, 3 * rows), 1), rows)
            last = lax.broadcasted_iota(jnp.int32, (rows, 3 * rows), 1) >= 2 * rows
            offset = source - target
            for at, value in enumerate(
                (second(offset), first(offset), first_extended(source, target, rows))
            ):
                high, low = split(value)
                left[at * rows : (at + 1) * rows] = jnp.where(
                    last, low.astype(jnp.float32), high.astype(jnp.float32)
                ).astype(jnp.bfloat16)

        def dot(a, b):
            return lax.dot_general(
                a, b, (((1,), (0,)), ((), ())), preferred_element_type=jnp.float32
            )

        def differences(value, which):
            high, low = split(value)
            flat_high = high.reshape(2 * rows, lanes)
            flat = jnp.concatenate([flat_high, low.reshape(2 * rows, lanes)], axis=1)
            first_column, columns = (0, 2 * lanes) if which == 0 else (2 * lanes, lanes)
            use = pl.ds(first_column, columns)
            along_y = dot(flat, right[0 : 2 * lanes, use]) + dot(
                flat_high, right[2 * lanes : 3 * lanes, use]
            )
            stacked = jnp.concatenate(
                [jnp.concatenate([high[i], low[i], high[i]], axis=0) for i in range(2)], axis=1
            )
            use = pl.ds(0, 2 * rows) if which == 0 else pl.ds(2 * rows, rows)
            along_x = dot(left[use], stacked)
            return along_x, along_y

        def inject():
            local_cells = cells_ref[...] - dom * (depth * plane)
            cell_rows = jnp.right_shift(local_cells, 7)
            cell_lanes = jnp.bitwise_and(local_cells, lanes - 1)
            lane_hot = lax.broadcasted_iota(jnp.int32, (lanes, receivers), 0) == cell_lanes
            amounts = jnp.concatenate(
                [jnp.where(lane_hot, traces_ref[0, k : k + 1, :], 0.0) for k in range(2)], axis=0
            )
            amounts = amounts.T
            high, _ = split(amounts)
            middle, low = split(amounts - high.astype(jnp.float32))
            row = lax.broadcasted_iota(jnp.int32, (depth * rows, receivers), 0)
            row_hot = jnp.where(row == cell_rows, 1.0, 0.0).astype(jnp.bfloat16)
            injected[...] = dot(row_hot, low) + dot(row_hot, middle) + dot(row_hot, high)

        def scale(z, carry):
            fields[SQ_NOW, WIDTH + z] = stiff[z] * adj[z]
            return carry

        bands = [lax.rem(column + i, 2) for i in range(2)]

        def far_ends(f, part, sending):
            of = band_rows(part)
            if f < 4:
                return far_halo.at[f, pl.ds(0, half), of]
            at = 1 - core if sending else core
            return buoy.at[pl.ds(at * (WIDTH + depth), half), of]

        def far_copy(f, part):
            src = (buoy if f == 4 else fields.at[f]).at[pl.ds(WIDTH + outer, half), band_rows(part)]
            return pltpu.make_async_remote_copy(
                src, far_ends(f, part, True), far_send.at[f, part], far_recv.at[f, part],
                device_id={"dom": far}, device_id_type=MESH,
            )

        def far_arrival(f, part):
            dst = far_ends(f, part, False)
            return pltpu.make_async_remote_copy(
                dst, dst, far_send.at[f, part], far_recv.at[f, part],
                device_id={"dom": far}, device_id_type=MESH,
            )

        def pass_on(part):
            ends = far_ends(4, part, False)
            return pltpu.make_async_remote_copy(
                ends, ends, pass_send, pass_recv,
                device_id={"shot": row * length + column + 1 - 2 * lax.rem(column, 2)}, device_id_type=MESH,
            )

        def near_copy(f):
            if f == 4:
                src = buoy.at[pl.ds(WIDTH + inner, half)]
                dst = buoy.at[pl.ds(core * (WIDTH + depth), half)]
            else:
                src = fields.at[f, pl.ds(WIDTH + inner, half)]
                dst = near_halo.at[f]
            return pltpu.make_async_remote_copy(
                src, dst, near_send.at[f], near_recv.at[f], device_id={"dom": near}, device_id_type=MESH
            )

        def near_arrival(f):
            if f == 4:
                dst = buoy.at[pl.ds((1 - core) * (WIDTH + depth), half)]
            else:
                dst = near_halo.at[f]
            return pltpu.make_async_remote_copy(
                dst, dst, near_send.at[f], near_recv.at[f], device_id={"dom": near}, device_id_type=MESH
            )

        def when_far(act):
            pl.when(has_far)(act)

        def buoy_slopes():
            for z in range(0, depth, 2):
                along_x, along_y = differences(buoy[WIDTH + z : WIDTH + z + 2], 1)
                for i in range(2):
                    slopes[0, z + i] = along_x[:, i * lanes : (i + 1) * lanes]
                    slopes[1, z + i] = along_y[i * rows : (i + 1) * rows]

        def buoy_slope_z(start, use):
            def body(j, carry):
                z = start + j
                along_z = jnp.zeros((use.size, lanes), jnp.float32)
                for k in range(1, 5):
                    up = buoy[WIDTH + z + k, use]
                    down = buoy[WIDTH + z - k, use]
                    along_z = along_z + C_FIRST[k - 1] * (up - down)
                slopes[2, z, use] = along_z
                return carry

            lax.fori_loop(0, half, body, 0)

        def local(f):
            for z0 in range(0, depth, 2):
                along_x, along_y = differences(fields[f, WIDTH + z0 : WIDTH + z0 + 2], 0)
                for i in range(2):
                    z = z0 + i
                    of_x = slice(i * lanes, (i + 1) * lanes)
                    of_y = slice(i * rows, (i + 1) * rows)
                    curve = along_x[0:rows, of_x] + along_y[of_y, 0:lanes]
                    along = jnp.zeros((rows, lanes), jnp.float32)
                    for k in range(1, 5):
                        up = fields[f, WIDTH + z + k]
                        down = fields[f, WIDTH + z - k]
                        curve = curve + C_SECOND[k] * (up + down)
                        along = along + C_FIRST[k - 1] * (up - down)
                    slope_z[f, z] = along
                    base[f, z] = (
                        buoy[WIDTH + z] * curve
                        + along_x[rows : 2 * rows, of_x] * slopes[0, z]
                        + along_y[of_y, lanes : 2 * lanes] * slopes[1, z]
                    )

        make_matrices()
        loads[0].wait()
        loads[1].wait()
        pl.semaphore_wait(barrier, len(steps) + 1 + far_count + (1 - core))

        when_far(far_copy(4, bands[0]).start)
        for part in bands:
            when_far(far_copy(P_NOW, part).start)
        loads[2].wait()
        loads[3].wait()
        lax.fori_loop(0, depth, scale, 0)
        for part in bands:
            when_far(far_copy(SQ_NOW, part).start)

        def near_begin():
            @pl.when(core == 0)
            def _():
                pl.semaphore_signal(near_ready, 1, device_id={"dom": near}, device_id_type=MESH)

            @pl.when(core == 1)
            def _():
                pl.semaphore_wait(near_ready, 1)

            for f in (4, P_NOW, SQ_NOW):
                near_copy(f).start()

        pl.when(dom != 1)(near_begin)
        for i in steps:
            pl.semaphore_signal(greeted.at[0], 1, device_id=along(i), device_id_type=MESH)

        buoy_slopes()
        local(P_NOW)
        local(SQ_NOW)
        loads[6].wait()
        loads[7].wait()
        inject()

        @pl.when(jnp.logical_not(has_far))
        def _():
            edge = buoy[WIDTH + core * (depth - 1)]
            for z in range(half):
                buoy[core * (WIDTH + depth) + z] = edge
                for f in range(4):
                    far_halo[f, z] = blank

        def whole(f, j, is_far, use):
            halo = far_halo if is_far else near_halo
            up = core if is_far else 1 - core
            z = up * (depth - 1 - j) + (1 - up) * j
            curve = jnp.zeros((use.size, lanes), jnp.float32)
            along = jnp.zeros((use.size, lanes), jnp.float32)
            for k in range(j + 1, 5):
                m = k - j
                plane_at = up * (m - 1) + (1 - up) * (half - m)
                value = halo[f, plane_at, use]
                curve = curve + C_SECOND[k] * value
                along = along + C_FIRST[k - 1] * value
            sign = side if is_far else -side
            along = slope_z[f, z, use] + sign * along
            value = base[f, z, use] + buoy[WIDTH + z, use] * curve + along * slopes[2, z, use]
            return z, value

        for i in (4, 5, 8, 9):
            loads[i].wait()
        local_source = source_ref[0] - dom * (depth * plane)
        amplitude = wavelet_ref[0, 0]
        everything = pl.ds(0, rows)

        def flat_rows(z, use):
            return pl.ds(pl.multiple_of(z * rows + use.start, band), use.size)

        def forward(is_far, use=everything):
            cell = lax.broadcasted_iota(jnp.int32, (use.size, lanes), 0) * lanes
            cell = cell + lax.broadcasted_iota(jnp.int32, (use.size, lanes), 1)
            for j in range(half):
                z, value = whole(P_NOW, j, is_far, use)
                image[z, use] = value
                here = cell + (z * plane + use.start * lanes)
                shown = jnp.where(here == local_source, amplitude, 0.0)
                fields[P_NEXT, WIDTH + z, use] = (
                    2.0 * fields[P_NOW, WIDTH + z, use] - prior[z, use] + stiff[z, use] * value + shown
                )

        def backward(is_far, use=everything):
            for j in range(half):
                z, value = whole(SQ_NOW, j, is_far, use)
                injected_rows = flat_rows(z, use)
                value = 2.0 * adj[z, use] - after[z, use] + value + injected[injected_rows, 0:lanes]
                adj_next[z, use] = value
                fields[SQ_NEXT, WIDTH + z, use] = stiff[z, use] * value

        def finish(is_far, use=everything):
            for j in range(half):
                z, last_image = whole(P_NEXT, j, is_far, use)
                _, value = whole(SQ_NEXT, j, is_far, use)
                newer = adj_next[z, use]
                flat = flat_rows(z, use)
                value = 2.0 * newer - adj[z, use] + value + injected[flat, lanes : 2 * lanes]
                grad[flat] = newer * last_image + value * image[z, use]

        def share(h, of_row, of_column):
            if h == 0:
                return pl.ds(inner * rows + (of_row * length + of_column) * chunk, chunk)
            at = of_column * chunk
            return pl.ds((outer + at // band) * rows + of_row * band + lax.rem(at, band), chunk)

        def share_copy(h, stage, to_row, i):
            to_column = lax.rem(column + i, length)
            if stage == 0:
                src, dst = grad.at[share(h, to_row, to_column)], parts.at[h, shot]
            else:
                src, dst = sums.at[h], out_ref.at[share(h, row, column)]
            return pltpu.make_async_remote_copy(
                src, dst, share_send.at[h, stage], share_recv.at[h, stage],
                device_id={"shot": to_row * length + to_column}, device_id_type=MESH,
            )

        def share_start(h, stage, to_row):
            for i in line:
                share_copy(h, stage, to_row, i).start()
            pl.when(row != to_row)(share_copy(h, stage, to_row, 0).start)

        def all_shares(h, stage):
            every = parts.at[h, pl.ds(0, shots - 1)]
            return pltpu.make_async_remote_copy(
                every, every, share_send.at[h, stage], share_recv.at[h, stage], device_id=across, device_id_type=MESH
            )

        def add_shares(h):
            all_shares(h, 0).wait_recv()
            total = grad[share(h, row, column)]
            for i in range(1, shots):
                total = total + parts[h, lax.rem(shot + i, shots)]
            sums[h] = total
            share_copy(h, 1, 1 - row, length // 2).start()
            for i in line:
                share_copy(h, 1, row, i).start()
                if i != length // 2:
                    share_copy(h, 1, 1 - row, i).start()
            share_copy(h, 1, 1 - row, 0).start()
            pltpu.make_async_copy(sums.at[h], out_ref.at[share(h, row, column)], own_sem.at[h]).start()

        def wide_share(of):
            return pl.ds(inner * rows + of * wide, wide)

        def wide_copy(stage, i):
            peer = lax.rem(column + i, length)
            if stage == 0:
                src, dst = grad.at[wide_share(peer)], wide_parts.at[column]
            else:
                src, dst = wide_sums.at[2], out_ref.at[wide_share(column)]
            return pltpu.make_async_remote_copy(
                src, dst, wide_send.at[stage], wide_recv.at[stage], device_id=along(i), device_id_type=MESH
            )

        def all_wide(stage):
            every = wide_parts.at[pl.ds(0, length - 1)]
            return pltpu.make_async_remote_copy(
                every, every, wide_send.at[stage], wide_recv.at[stage], device_id=across, device_id_type=MESH
            )

        swap = pltpu.make_async_remote_copy(
            wide_sums.at[0], wide_sums.at[1], wide_send.at[2], wide_recv.at[2], device_id=across, device_id_type=MESH
        )

        def swap_wide():
            all_wide(0).wait_recv()
            total = grad[wide_share(column)]
            for i in line:
                total = total + wide_parts[lax.rem(column + i, length)]
            wide_sums[0] = total
            swap.start()

        def add_wide():
            swap.wait_recv()
            wide_sums[2] = wide_sums[0] + wide_sums[1]
            for i in reversed(line):
                wide_copy(1, i).start()
            pltpu.make_async_copy(wide_sums.at[2], out_ref.at[wide_share(column)], own_sem.at[2]).start()

        direct = dom < 2

        def near_fold():
            near_arrival(4).wait_recv()
            buoy_slope_z(inner, everything)
            near_arrival(P_NOW).wait_recv()
            forward(False)
            near_copy(P_NEXT).start()
            near_arrival(SQ_NOW).wait_recv()
            backward(False)
            near_copy(SQ_NEXT).start()

        pl.when(dom != 1)(near_fold)
        pl.semaphore_wait(greeted.at[0], len(steps))
        for i in leaps:
            pl.semaphore_signal(greeted.at[1], 1, device_id=along(i), device_id_type=MESH)
        when_far(far_arrival(4, bands[0]).wait_recv)
        when_far(pass_on(bands[0]).start)
        for part in bands:
            use = band_rows(part)
            if part is bands[1]:
                when_far(pass_on(part).wait_recv)
            buoy_slope_z(outer, use)
            when_far(far_arrival(P_NOW, part).wait_recv)
            forward(True, use)
            when_far(far_copy(P_NEXT, part).start)

        if leaps:
            pl.semaphore_wait(greeted.at[1], len(leaps))
        pl.semaphore_signal(greeted.at[2], 1, device_id=across, device_id_type=MESH)
        pl.when(dom != 1)(lambda: local(P_NEXT))

        for part in bands:
            when_far(far_arrival(SQ_NOW, part).wait_recv)
            backward(True, band_rows(part))
            when_far(far_copy(SQ_NEXT, part).start)

        @pl.when(dom == 1)
        def _():
            near_begin()
            near_fold()
            local(P_NEXT)

        local(SQ_NEXT)
        near_arrival(P_NEXT).wait_recv()
        near_arrival(SQ_NEXT).wait_recv()
        finish(False)

        pl.semaphore_wait(greeted.at[2], 1)

        @pl.when(direct)
        def _():
            for to_row in range(2):
                share_start(0, 0, to_row)

        @pl.when(jnp.logical_not(direct))
        def _():
            for i in line:
                wide_copy(0, i).start()


        for part in bands:
            when_far(far_arrival(P_NEXT, part).wait_recv)
            when_far(far_arrival(SQ_NEXT, part).wait_recv)
            finish(True, band_rows(part))
            share_start(1, 0, part)
            if part is bands[0]:
                pl.when(jnp.logical_not(direct))(swap_wide)

        @pl.when(direct)
        def _():
            add_shares(0)

        pl.when(jnp.logical_not(direct))(add_wide)
        add_shares(1)

        for f in range(5):
            for part in bands[: 1 if f == 4 else 2]:
                when_far(far_copy(f, part).wait_send)
            near_copy(f).wait_send()
        when_far(pass_on(bands[0]).wait_send)
        def drain(h):
            for stage in range(2):
                all_shares(h, stage).wait_send()
            pltpu.make_async_copy(sums.at[h], out_ref.at[share(h, row, column)], own_sem.at[h]).wait()
            all_shares(h, 1).wait_recv()

        @pl.when(direct)
        def _():
            drain(0)

        @pl.when(jnp.logical_not(direct))
        def _():
            for stage in range(2):
                all_wide(stage).wait_send()
            swap.wait_send()
            pltpu.make_async_copy(wide_sums.at[2], out_ref.at[wide_share(column)], own_sem.at[2]).wait()
            all_wide(1).wait_recv()

        drain(1)

    return kernel


def solution(mesh):
    shots, doms = mesh.shape["shot"], mesh.shape["dom"]

    def shards(
        stiffness,
        buoyancy,
        forward_now,
        forward_prior,
        adjoint_now,
        adjoint_after,
        source_cells,
        wavelet,
        receiver_cells,
        residuals,
    ):
        depth, rows, lanes = stiffness.shape
        receivers = receiver_cells.shape[1]
        half = depth // 2
        chunk = half * rows // shots
        wide = 2 * chunk
        padded = (depth + 2 * WIDTH, rows, lanes)
        slab = (depth, rows, lanes)
        f32 = jnp.float32
        in_hbm = pl.BlockSpec(memory_space=pltpu.HBM)
        in_any = pl.BlockSpec(memory_space=pl.ANY)
        return pl.pallas_call(
            make_kernel(shots, doms, depth, rows, lanes, receivers),
            out_shape=jax.ShapeDtypeStruct((depth * rows, lanes), f32),
            in_specs=[in_hbm] * 6 + [in_any] * 4,
            out_specs=in_any,
            scratch_shapes=[
                pltpu.SMEM((1,), jnp.int32),
                pltpu.SMEM((1, 1), f32),
                pltpu.VMEM((1, receivers), jnp.int32),
                pltpu.VMEM((1, 2, receivers), f32),
                pltpu.VMEM(padded, f32),
                pltpu.VMEM((4, *padded), f32),
                pltpu.VMEM(slab, f32),
                pltpu.VMEM(slab, f32),
                pltpu.VMEM(slab, f32),
                pltpu.VMEM(slab, f32),
                pltpu.VMEM((4, half, rows, lanes), f32),
                pltpu.VMEM((4, half, rows, lanes), f32),
                pltpu.VMEM((3, *slab), f32),
                pltpu.VMEM((4, *slab), f32),
                pltpu.VMEM((4, *slab), f32),
                pltpu.VMEM(slab, f32),
                pltpu.VMEM(slab, f32),
                pltpu.VMEM((depth * rows, 2 * lanes), f32),
                pltpu.VMEM((3 * rows, 3 * rows), jnp.bfloat16),
                pltpu.VMEM((3 * lanes, 3 * lanes), jnp.bfloat16),
                pltpu.VMEM((depth * rows, lanes), f32),
                pltpu.VMEM((2, shots, chunk, lanes), f32),
                pltpu.VMEM((2, chunk, lanes), f32),
                pltpu.SemaphoreType.DMA((10,)),
                pltpu.SemaphoreType.DMA((3,)),
                pltpu.SemaphoreType.DMA((5, 2)),
                pltpu.SemaphoreType.DMA((5, 2)),
                pltpu.SemaphoreType.DMA((5,)),
                pltpu.SemaphoreType.DMA((5,)),
                pltpu.SemaphoreType.DMA((2, 2)),
                pltpu.SemaphoreType.DMA((2, 2)),
                pltpu.VMEM((shots // 2, wide, lanes), f32),
                pltpu.VMEM((3, wide, lanes), f32),
                pltpu.SemaphoreType.DMA((3,)),
                pltpu.SemaphoreType.DMA((3,)),
                pltpu.SemaphoreType.REGULAR,
                pltpu.SemaphoreType.DMA,
                pltpu.SemaphoreType.DMA,
                pltpu.SemaphoreType.REGULAR((3,)),
            ],
            compiler_params=pltpu.CompilerParams(
                collective_id=0, has_side_effects=True, vmem_limit_bytes=54800 * 1024
            ),
            name="window",
        )(
            stiffness, buoyancy, forward_now, forward_prior, adjoint_now, adjoint_after,
            source_cells, wavelet, receiver_cells, residuals,
        ).reshape(slab)

    placed = (
        P("dom", None, None),
        P("dom", None, None),
        P("shot", "dom", None, None),
        P("shot", "dom", None, None),
        P("shot", "dom", None, None),
        P("shot", "dom", None, None),
        P("shot"),
        P("shot", None),
        P("shot", None),
        P("shot", None, None),
    )
    return jax.shard_map(
        shards, mesh=mesh, in_specs=placed, out_specs=P("dom", None, None), check_vma=False
    )
```
